128 devices in a mesh: wide: 16 (over y, x_lo, core), narrow: 8 (over x_hi, z).
Axes of the slice: x: 4 (x_hi: 2, x_lo: 2; x = x_hi * 2 + x_lo), y: 4, z: 4, core: 2. Of those that a mesh axis runs over, the one named last changes fastest.
Arguments:
- state: float32 [5, 2048, 4, 4096], P(None, ('wide', 'narrow')), may hold values from -3.75 to 46, as said below
Outputs:
- advanced: float32 [5, 2048, 4, 4096], P(None, ('wide', 'narrow'))
The draws below stay inside these ranges and needn't reach their ends.
Inputs may be any that keep to these rules, and one draw needn't show every extreme that they name: state holds density in [0.5, 2.5], momenta, and total energy whose pressure (gamma 1.4) lies in [0.4, 15].
All inputs are finite; a program needn't handle non-finite values. Where the reference program divides by a largest or mean magnitude, that divisor is 1e-20 or more.
Results may differ from the reference program's by a relative error of at most 0.0003.
Values sent between devices are 32-bit elements; how exact they have to be, the bound alone decides.
No kernel may reach another device: no remote copies, remote signals or barrier semaphores. Data moves between devices by JAX's collectives and lax.ppermute only.
A program may use at most 128 MiB of HBM per device.

```python
import math
import jax
import jax.numpy as jnp
from jax import lax

NX = 4096
NY = 2048
PLANES = 4


def draw_state(key, part):
    key_density = jax.random.fold_in(key, 11)
    key_velocity = jax.random.fold_in(key, 12)
    key_pressure = jax.random.fold_in(key, 13)
    shape = (NY, PLANES, NX)
    row_frac = (jnp.arange(NY, dtype=jnp.float32) / NY).reshape(NY, 1, 1)
    col_frac = (jnp.arange(NX, dtype=jnp.float32) / NX).reshape(1, 1, NX)
    pressure_scale = jnp.power(4.0, row_frac) * jnp.power(1.5, col_frac)
    density = jax.random.uniform(key_density, shape, jnp.float32, 0.5, 2.0)
    velocity = jnp.clip(0.5 * jax.random.normal(key_velocity, (3,) + shape, jnp.float32), -1.5, 1.5)
    pressure = jnp.exp(jax.random.uniform(key_pressure, shape, jnp.float32, math.log(0.4), math.log(2.5))) * pressure_scale
    energy = pressure / 0.4 + 0.5 * density * jnp.sum(velocity * velocity, axis=0)
    return jnp.concatenate([density[None], density[None] * velocity, energy[None]], 0).astype(jnp.float32)


def setup_inputs(seed: int = 0) -> dict:
    streams_of = jax.random.split(jax.random.key(seed), 2)
    return {
        "state": draw_state(jax.random.fold_in(streams_of[1], 71), 0),
    }


gamma_minus = 0.4
gamma_ratio = 1.4
courant_number = 0.6

def primitives(cons_vars):
    density = cons_vars[0]
    velocity = cons_vars[1:4] / density
    pressure = gamma_minus * (cons_vars[4] - 0.5 * density * lax.optimization_barrier(jnp.sum(velocity * velocity, axis=0)))
    return jnp.concatenate([density[None], velocity, pressure[None]], 0)

def euler_flux(prim_vars, normal):
    density = prim_vars[0]
    velocity = prim_vars[1:4]
    pressure = prim_vars[4]
    normal_speed = prim_vars[normal]
    momentum = density * velocity
    energy = pressure / gamma_minus + 0.5 * density * lax.optimization_barrier(jnp.sum(velocity * velocity, axis=0))
    cons_vars = jnp.concatenate([density[None], momentum, energy[None]], 0)
    components = [momentum[entry] * normal_speed + (pressure if entry == normal - 1 else 0.0) for entry in range(3)]
    fluxes = jnp.stack([density * normal_speed] + components + [(energy + pressure) * normal_speed], 0)
    signal = jnp.abs(normal_speed) + jnp.sqrt(gamma_ratio * pressure / density)
    return (cons_vars, fluxes, signal)

def ppm_sweep(padded, sweep_axis, normal, time_step):
    length = padded.shape[sweep_axis]

    def take_slice(values, start, limit):
        return lax.slice_in_dim(values, start, limit, axis=sweep_axis)
    prim_vars = primitives(padded)
    jumps = take_slice(prim_vars, 1, length) - take_slice(prim_vars, 0, length - 1)
    back_jump = take_slice(jumps, 0, length - 2)
    fore_jump = take_slice(jumps, 1, length - 1)
    centred = 0.5 * (back_jump + fore_jump)
    magnitude = jnp.minimum(jnp.abs(centred), 2.0 * jnp.minimum(jnp.abs(back_jump), jnp.abs(fore_jump)))
    slopes = jnp.where(back_jump * fore_jump > 0, jnp.sign(centred) * magnitude, 0.0)
    faces = 0.5 * (take_slice(prim_vars, 1, length - 2) + take_slice(prim_vars, 2, length - 1)) - (take_slice(slopes, 1, length - 2) - take_slice(slopes, 0, length - 3)) / 6.0
    centre = take_slice(prim_vars, 2, length - 2)
    left_edge = take_slice(faces, 0, length - 4)
    right_edge = take_slice(faces, 1, length - 3)
    flatten = (right_edge - centre) * (centre - left_edge) <= 0
    edge_gap = right_edge - left_edge
    offset = centre - 0.5 * (left_edge + right_edge)
    left_new = jnp.where(edge_gap * offset > edge_gap * edge_gap / 6.0, 3.0 * centre - 2.0 * right_edge, left_edge)
    right_new = jnp.where(-edge_gap * edge_gap / 6.0 > edge_gap * offset, 3.0 * centre - 2.0 * left_edge, right_edge)
    left_edge = jnp.where(flatten, centre, left_new)
    right_edge = jnp.where(flatten, centre, right_new)
    courant = time_step * (jnp.abs(centre[normal]) + jnp.sqrt(gamma_ratio * centre[4] / centre[0]))[None]
    edge_gap = right_edge - left_edge
    curvature = 6.0 * (centre - 0.5 * (left_edge + right_edge))
    shrink = 1.0 - 2.0 * courant / 3.0
    to_right = right_edge - 0.5 * courant * (edge_gap - shrink * curvature)
    to_left = left_edge + 0.5 * courant * (edge_gap + shrink * curvature)
    left_cons, left_flux, left_speed = euler_flux(take_slice(to_right, 0, length - 5), normal)
    right_cons, right_flux, right_speed = euler_flux(take_slice(to_left, 1, length - 4), normal)
    fluxes = 0.5 * (left_flux + right_flux) - 0.5 * jnp.maximum(left_speed, right_speed)[None] * (right_cons - left_cons)
    interior = take_slice(padded, 3, length - 3)
    return interior - time_step * (take_slice(fluxes, 1, length - 5) - take_slice(fluxes, 0, length - 6))

def wrap_pad(values, sweep_axis):
    extent = values.shape[sweep_axis]
    return jnp.concatenate([lax.slice_in_dim(values, extent - 3, extent, axis=sweep_axis), values, lax.slice_in_dim(values, 0, 3, axis=sweep_axis)], sweep_axis)

def reference(state):
    prim_vars = primitives(state)
    sound = jnp.sqrt(gamma_ratio * prim_vars[4] / prim_vars[0])
    peak_speed = jnp.max(jnp.maximum(jnp.abs(prim_vars[1]), jnp.abs(prim_vars[2])) + sound)
    time_step = courant_number / peak_speed

    def one_plane(plane_state):
        plane_state = ppm_sweep(wrap_pad(plane_state, 2), 2, 1, 0.5 * time_step)
        plane_state = ppm_sweep(wrap_pad(plane_state, 1), 1, 2, time_step)
        plane_state = ppm_sweep(wrap_pad(plane_state, 2), 2, 1, 0.5 * time_step)
        return plane_state
    advanced = lax.map(one_plane, jnp.moveaxis(state, 2, 0))
    return jnp.moveaxis(advanced, 0, 2)
```

```python
import jax
import jax.numpy as jnp
from jax import lax
from jax.experimental import pallas as pl
from jax.experimental.pallas import tpu as pltpu
from jax.sharding import Mesh
from jax.sharding import PartitionSpec as P

WIDE_NARROW = ("wide_0", "wide_1", "wide_2", "narrow_0", "narrow_1")

gamma_minus = 0.4
root_gamma = 1.4**0.5
courant_number = 0.6
smallest = 1e-30

FIELDS = 5
HALO = 3
SEGMENT = 16


def sound_speed(density, pressure):
    return root_gamma * (pressure * lax.rsqrt(jnp.maximum(pressure * density, smallest)))


def primitives(cons):
    density, mom_x, mom_y, mom_z, energy = cons
    inverse = 1.0 / density
    vel_x, vel_y, vel_z = mom_x * inverse, mom_y * inverse, mom_z * inverse
    kinetic = mom_x * vel_x + mom_y * vel_y + mom_z * vel_z
    pressure = gamma_minus * energy - (0.5 * gamma_minus) * kinetic
    return [density, vel_x, vel_y, vel_z, pressure]


def next_segment(value):
    moved = pltpu.roll(value, 7, 0)
    sub = lax.broadcasted_iota(jnp.int32, value.shape, 0)
    return jnp.where(sub == 7, pltpu.roll(moved, 124, 1), moved)


def last_segment(value):
    moved = pltpu.roll(value, 1, 0)
    sub = lax.broadcasted_iota(jnp.int32, value.shape, 0)
    return jnp.where(sub == 0, pltpu.roll(moved, 4, 1), moved)


def jump_of(here, there):
    jump = there - here
    return jnp.abs(jump), jnp.where(jump > 0, 0.5, -0.5)


def slope_of(back, fore):
    sign = back[1] + fore[1]
    size = jnp.minimum(back[0] + fore[0], 4.0 * jnp.minimum(back[0], fore[0]))
    return size * jnp.abs(sign), sign


def edges_of(jump, here, there):
    turn = there[0] - here[0]
    base = 6.0 * jump[0]
    return base - turn, base + turn


def limit(right, left, sign):
    return jnp.minimum(right, 2.0 * left) * sign, jnp.minimum(left, 2.0 * right) * sign


def reconstruct(line, store, count, wrap):
    if wrap:
        jumps = {}
        jumps[count - 1] = jump_of(line(count - 1), next_segment(line(0)))
        jumps[-1] = (last_segment(jumps[count - 1][0]), last_segment(jumps[count - 1][1]))
        slopes = {}
        edges = {}
        for k in range(count):
            if k < count - 1:
                jumps[k] = jump_of(line(k), line(k + 1))
            slopes[k] = slope_of(jumps[k - 1], jumps[k])
            if k >= 1:
                edges[k - 1] = edges_of(jumps[k - 1], slopes[k - 1], slopes[k])
            if k >= 2:
                store(k - 1, limit(edges[k - 1][0], edges[k - 2][1], slopes[k - 1][1]))
        slope_next = (next_segment(slopes[0][0]),)
        edges[count - 1] = edges_of(jumps[count - 1], slopes[count - 1], slope_next)
        store(count - 1, limit(edges[count - 1][0], edges[count - 2][1], slopes[count - 1][1]))
        store(0, limit(edges[0][0], last_segment(edges[count - 1][1]), slopes[0][1]))
        return
    jumps = {-3: jump_of(line(-3), line(-2))}
    slopes, edges = {}, {}
    for k in range(-2, count + 2):
        jumps[k] = jump_of(line(k), line(k + 1))
        slopes[k] = slope_of(jumps[k - 1], jumps[k])
        if k >= -1:
            edges[k - 1] = edges_of(jumps[k - 1], slopes[k - 1], slopes[k])
        if k >= 0:
            store(k - 1, limit(edges[k - 1][0], edges[k - 2][1], slopes[k - 1][1]))


def rusanov(before, behind, normal):
    vn_l, vn_r = before[normal], behind[normal]
    speed = jnp.maximum(
        jnp.abs(vn_l) + sound_speed(before[0], before[4]),
        jnp.abs(vn_r) + sound_speed(behind[0], behind[4]),
    )
    rate_l, rate_r = vn_l + speed, vn_r - speed
    mass_l, mass_r = before[0] * rate_l, behind[0] * rate_r
    mom_l = [before[i] * mass_l for i in (1, 2, 3)]
    mom_r = [behind[i] * mass_r for i in (1, 2, 3)]
    kinetic = (
        (before[1] * mom_l[0] + before[2] * mom_l[1])
        + (before[3] * mom_l[2] + behind[1] * mom_r[0])
        + (behind[2] * mom_r[1] + behind[3] * mom_r[2])
    )
    flux = [mass_l + mass_r] + [mom_l[i] + mom_r[i] for i in range(3)]
    flux[normal] = flux[normal] + (before[4] + behind[4])
    flux.append(
        0.5 * kinetic
        + (before[4] * (2.5 * rate_l + vn_l) + behind[4] * (2.5 * rate_r + vn_r))
    )
    return flux


def march(prim, edge, courant, cons, put, count, normal, half_step, wrap):
    def faces(k):
        sigma, scale = courant(k)
        right, left = [], []
        for f in range(FIELDS):
            value = prim(f, k)
            dist_r, dist_l = edge(f, k)
            mixed = sigma * (dist_r - dist_l)
            right.append(value + scale * (dist_r - mixed))
            left.append(value - scale * (dist_l + mixed))
        return right, left

    def update(k, low, high):
        old = cons(k)
        put(k, [old[f] - half_step * (high[f] - low[f]) for f in range(FIELDS)])

    if wrap:
        right, first_left = faces(0)
        fluxes = {}
        for k in range(count):
            if k < count - 1:
                right_next, left = faces(k + 1)
            else:
                left = [next_segment(v) for v in first_left]
            fluxes[k] = rusanov(right, left, normal)
            if k >= 1:
                update(k, fluxes[k - 1], fluxes[k])
            right = right_next
        update(0, [last_segment(v) for v in fluxes[count - 1]], fluxes[0])
        return
    right, _ = faces(-1)
    low = None
    for k in range(0, count + 1):
        right_next, left = faces(k)
        high = rusanov(right, left, normal)
        if low is not None:
            update(k - 1, low, high)
        low, right = high, right_next


def sweep_line(cons, put, prim_ref, edge_ref, courant_ref, count, normal, step, wrap):
    pad = 0 if wrap else HALO
    for k in range(-pad, count + pad):
        prim = primitives(cons(k))
        for f in range(FIELDS):
            prim_ref[f, k + pad] = prim[f]
        if wrap or -1 <= k <= count:
            sigma = step * (jnp.abs(prim[normal]) + sound_speed(prim[0], prim[4]))
            courant_ref[0, k + pad] = sigma
            courant_ref[1, k + pad] = (1.0 - sigma) * (1.0 / 12.0)

    for f in range(FIELDS):

        def store(k, pair, f=f):
            edge_ref[0, f, k + pad], edge_ref[1, f, k + pad] = pair

        reconstruct(lambda k, f=f: prim_ref[f, k + pad], store, count, wrap)

    march(
        lambda f, k: prim_ref[f, k + pad],
        lambda f, k: (edge_ref[0, f, k + pad], edge_ref[1, f, k + pad]),
        lambda k: (courant_ref[0, k + pad], courant_ref[1, k + pad]),
        cons,
        put,
        count,
        normal,
        0.5 * step,
        wrap,
    )


def peak_kernel(state_ref, peak_ref):
    def body(i, best):
        for half in range(4):
            rows = pl.ds(pl.multiple_of(i * 32 + half * 8, 8), 8)
            prim = primitives([state_ref[f, 0, rows, :] for f in range(FIELDS)])
            sound = sound_speed(prim[0], prim[4])
            best = jnp.maximum(best, jnp.maximum(jnp.abs(prim[1]), jnp.abs(prim[2])) + sound)
        return best

    best = lax.fori_loop(0, 4, body, jnp.zeros((8, 128), jnp.float32))

    @pl.when(pl.program_id(0) == 0)
    def _():
        peak_ref[...] = best

    @pl.when(pl.program_id(0) > 0)
    def _():
        peak_ref[...] = jnp.maximum(peak_ref[...], best)


def peak_call(view):
    rows = view.shape[1]
    return pl.pallas_call(
        peak_kernel,
        grid=(rows,),
        in_specs=[pl.BlockSpec((FIELDS, 1, 128, 128), lambda i: (0, i, 0, 0))],
        out_specs=pl.BlockSpec((8, 128), lambda i: (0, 0)),
        out_shape=jax.ShapeDtypeStruct((8, 128), jnp.float32),
        name="peak",
    )(view)


def window_kernel(
    state_ref, low_ref, high_ref, peaks_ref, out_ref, swept, done, turned, back, prim, edge, courant
):
    rows = state_ref.shape[1]
    peak = jnp.max(peaks_ref[...])
    step = courant_number / jnp.full((8, 128), peak, jnp.float32)
    half = 0.5 * step

    def first_sweep(source, source_row, row):
        for f in range(FIELDS):
            turned[f] = source[f, source_row].T

        def cons(k):
            return [turned[f, pl.ds(k, 8, stride=SEGMENT), :] for f in range(FIELDS)]

        def put(k, new):
            for f in range(FIELDS):
                swept[f, row, k] = new[f]

        sweep_line(cons, put, prim, edge, courant, SEGMENT, 1, half, True)

    def low_body(i, carry):
        first_sweep(low_ref, i, i)
        return carry

    def high_body(i, carry):
        first_sweep(high_ref, i, i + HALO + rows)
        return carry

    def state_body(i, carry):
        first_sweep(state_ref, i, i + HALO)
        return carry

    lax.fori_loop(0, HALO, low_body, 0)
    lax.fori_loop(0, rows, state_body, 0)
    lax.fori_loop(0, HALO, high_body, 0)

    def column(t, carry):
        def cons(k):
            return [swept[f, k + HALO, t] for f in range(FIELDS)]

        def put(k, new):
            for f in range(FIELDS):
                done[f, k, t] = new[f]

        sweep_line(cons, put, prim, edge, courant, rows, 2, step, False)
        return carry

    lax.fori_loop(0, SEGMENT, column, 0)

    def last_sweep(i, carry):
        def cons(k):
            return [done[f, i, k] for f in range(FIELDS)]

        def put(k, new):
            for f in range(FIELDS):
                back[f, pl.ds(k, 8, stride=SEGMENT), :] = new[f]

        sweep_line(cons, put, prim, edge, courant, SEGMENT, 1, half, True)
        for f in range(FIELDS):
            out_ref[f, i] = back[f].T
        return carry

    lax.fori_loop(0, rows, last_sweep, 0)


def window_call(view, low, high, peaks):
    rows = view.shape[1]
    padded = rows + 2 * HALO
    return pl.pallas_call(
        window_kernel,
        in_specs=[pl.BlockSpec(memory_space=pltpu.VMEM)] * 4,
        out_specs=pl.BlockSpec(memory_space=pltpu.VMEM),
        out_shape=jax.ShapeDtypeStruct(view.shape, jnp.float32),
        scratch_shapes=[
            pltpu.VMEM((FIELDS, padded, SEGMENT, 8, 128), jnp.float32),
            pltpu.VMEM((FIELDS, rows, SEGMENT, 8, 128), jnp.float32),
            pltpu.VMEM((FIELDS, 128, 128), jnp.float32),
            pltpu.VMEM((FIELDS, 128, 128), jnp.float32),
            pltpu.VMEM((FIELDS, padded, 8, 128), jnp.float32),
            pltpu.VMEM((2, FIELDS, padded, 8, 128), jnp.float32),
            pltpu.VMEM((2, padded, 8, 128), jnp.float32),
        ],
        compiler_params=pltpu.CompilerParams(vmem_limit_bytes=56 * 1024 * 1024),
        name="window",
    )(view, low, high, peaks)


def local(state):
    fields, rows, planes, columns = state.shape
    tiles = columns // 128
    view = state.reshape(fields, rows, planes, tiles, 128).transpose(0, 1, 3, 2, 4)
    view = view.reshape(fields, rows, tiles * planes, 128)
    devices = 1
    for axis in WIDE_NARROW:
        devices *= lax.axis_size(axis)
    up = [(i, (i + 1) % devices) for i in range(devices)]
    low = lax.ppermute(view[:, rows - HALO :], WIDE_NARROW, up)
    high = lax.ppermute(view[:, :HALO], WIDE_NARROW, [(b, a) for a, b in up])
    peak = jnp.max(peak_call(view), axis=0, keepdims=True)
    peaks = lax.all_to_all(
        jnp.broadcast_to(peak, (devices, 128)), WIDE_NARROW, 0, 0, tiled=True
    )
    out = window_call(view, low, high, peaks)
    out = out.reshape(fields, rows, tiles, planes, 128).transpose(0, 1, 3, 2, 4)
    return out.reshape(fields, rows, planes, columns)


def solution(mesh):
    split = Mesh(
        mesh.devices.reshape(4, 2, 2, 2, 4), ("wide_0", "wide_1", "wide_2", "narrow_0", "narrow_1")
    )
    placed = (P(None, WIDE_NARROW, None, None),)
    return jax.shard_map(
        local,
        mesh=split,
        in_specs=placed,
        out_specs=P(None, WIDE_NARROW, None, None),
        check_vma=False,
    )
```

```python
import jax
import jax.numpy as jnp
from jax import lax
from jax.experimental import pallas as pl
from jax.experimental.pallas import tpu as pltpu
from jax.sharding import Mesh
from jax.sharding import PartitionSpec as P

WIDE_NARROW = ("wide_0", "wide_1", "wide_2", "narrow_0", "narrow_1")

gamma_minus = 0.4
root_gamma = 1.4**0.5
courant_number = 0.6
smallest = 1e-30

FIELDS = 5
HALO = 3
SEGMENT = 16


def sound_speed(density, pressure, scale=1.0):
    return (root_gamma * scale) * (
        pressure * lax.rsqrt(jnp.maximum(pressure * density, smallest))
    )


def primitives(cons):
    density, mom_x, mom_y, mom_z, energy = cons
    inverse = 1.0 / density
    vel_x, vel_y, vel_z = mom_x * inverse, mom_y * inverse, mom_z * inverse
    kinetic = mom_x * vel_x + mom_y * vel_y + mom_z * vel_z
    pressure = gamma_minus * energy - (0.5 * gamma_minus) * kinetic
    return [density, vel_x, vel_y, vel_z, pressure]


def next_segment(value):
    moved = pltpu.roll(value, 7, 0)
    sub = lax.broadcasted_iota(jnp.int32, value.shape, 0)
    return jnp.where(sub == 7, pltpu.roll(moved, 124, 1), moved)


def last_segment(value):
    moved = pltpu.roll(value, 1, 0)
    sub = lax.broadcasted_iota(jnp.int32, value.shape, 0)
    return jnp.where(sub == 0, pltpu.roll(moved, 4, 1), moved)


class Lazy(dict):
    def __init__(self, make):
        super().__init__()
        self.make = make

    def __missing__(self, k):
        value = self[k] = self.make(k)
        return value


def make_reconstruct(cell, courant):
    def jump(k):
        step = cells[k + 1] - cells[k]
        return jnp.abs(step), step > 0

    def slope(k):
        (back, back_up), (fore, fore_up) = jumps[k - 1], jumps[k]
        turns = jnp.logical_xor(back_up, fore_up)
        size = jnp.minimum(back + fore, 4.0 * jnp.minimum(back, fore))
        return jnp.where(turns, 0.0, size), turns

    def edge(k):
        turn = slopes[k + 1][0] - slopes[k][0]
        base = 6.0 * jumps[k][0]
        return base - turn, base + turn

    def faces(k):
        right, left = edges[k][0], edges[k - 1][1]
        right, left = jnp.minimum(right, 2.0 * left), jnp.minimum(left, 2.0 * right)
        sigma, scale = courant(k)
        signed = jnp.where(slopes[k][1], 0.0, jnp.where(jumps[k][1], scale, -scale))
        mixed = sigma * (right - left)
        return cells[k] + signed * (right - mixed), cells[k] - signed * (left + mixed)

    cells, jumps, slopes, edges = Lazy(cell), Lazy(jump), Lazy(slope), Lazy(edge)
    return faces


def rusanov(before, behind, normal, step):
    half = 0.5 * step
    vn_l, vn_r = half * before[normal], half * behind[normal]
    speed = jnp.maximum(
        jnp.abs(vn_l) + sound_speed(before[0], before[4], half),
        jnp.abs(vn_r) + sound_speed(behind[0], behind[4], half),
    )
    rate_l, rate_r = vn_l + speed, vn_r - speed
    mass_l, mass_r = before[0] * rate_l, behind[0] * rate_r
    mom_l = [before[i] * mass_l for i in (1, 2, 3)]
    mom_r = [behind[i] * mass_r for i in (1, 2, 3)]
    kinetic = (
        (before[1] * mom_l[0] + before[2] * mom_l[1])
        + (before[3] * mom_l[2] + behind[1] * mom_r[0])
        + (behind[2] * mom_r[1] + behind[3] * mom_r[2])
    )
    flux = [mass_l + mass_r] + [mom_l[i] + mom_r[i] for i in range(3)]
    flux[normal] = flux[normal] + half * (before[4] + behind[4])
    flux.append(
        0.5 * kinetic
        + (before[4] * (2.5 * rate_l + vn_l) + behind[4] * (2.5 * rate_r + vn_r))
    )
    return flux


def sweep_line(cons, put, scratch, count, normal, step, wrap, beside=None):
    prim_ref, face_ref, courant_ref = scratch
    first = 0 if wrap else -HALO
    last = count if wrap else count + HALO
    reach = HALO

    def start(k):
        prim = primitives(cons(k))
        for f in range(FIELDS):
            prim_ref[f, k + reach] = prim[f]
        if wrap or -1 <= k <= count:
            sigma = step * jnp.abs(prim[normal]) + sound_speed(prim[0], prim[4], step)
            courant_ref[0, k + reach] = sigma
            courant_ref[1, k + reach] = (1.0 / 12.0) - (1.0 / 12.0) * sigma
        return prim

    if wrap:
        for k in (0, 1):
            prim = start(k)
            for f in range(FIELDS):
                prim_ref[f, count + k + reach] = next_segment(prim[f])
        for k in (count - 2, count - 1):
            prim = start(k)
            for f in range(FIELDS):
                prim_ref[f, k - count + reach] = last_segment(prim[f])
        for k in range(2, count - 2):
            start(k)
        order = [*range(2, count), 0, 1]
    else:
        for k in range(first, last):
            start(k)
        order = list(range(-1, count + 1))

    for f in range(FIELDS):
        if beside is not None:
            beside(f)
        faces = make_reconstruct(
            lambda k, f=f: prim_ref[f, k + reach],
            lambda k: (courant_ref[0, k + reach], courant_ref[1, k + reach]),
        )
        for k in order:
            face_ref[0, f, k + reach], face_ref[1, f, k + reach] = faces(k)

    def flux(k, behind=None):
        before = [face_ref[0, f, k + reach] for f in range(FIELDS)]
        if behind is None:
            behind = [face_ref[1, f, k + 1 + reach] for f in range(FIELDS)]
        return rusanov(before, behind, normal, step)

    def update(k, low, high):
        old = cons(k)
        put(k, [old[f] + (low[f] - high[f]) for f in range(FIELDS)])

    if wrap:
        behind = [next_segment(face_ref[1, f, reach]) for f in range(FIELDS)]
        front = low = flux(0)
        middle = count // 2
        for k in range(1, count):
            if k == middle:
                end = flux(count - 1, behind)
                into = [last_segment(v) for v in end]
            high = flux(k) if k < count - 1 else end
            update(k, low, high)
            low = high
        update(0, into, front)
        return
    low = flux(-1)
    for k in range(count):
        high = flux(k)
        update(k, low, high)
        low = high


PEAK_STEPS = 4


def peak_kernel(state_ref, peak_ref, best_ref):
    rows = state_ref.shape[1]
    place = pl.program_id(0)

    def body(i, best):
        best = list(best)
        for row in range(rows):
            at = pl.ds(pl.multiple_of(i * 8, 8), 8)
            prim = primitives([state_ref[f, row, at, :] for f in range(FIELDS)])
            sound = sound_speed(prim[0], prim[4])
            new = jnp.maximum(jnp.abs(prim[1]), jnp.abs(prim[2])) + sound
            best[row] = jnp.maximum(best[row], new)
        return tuple(best)

    zero = jnp.zeros((8, 128), jnp.float32)
    parts = lax.fori_loop(0, 16, body, (zero,) * rows, unroll=4)
    best = parts[0]
    for part in parts[1:]:
        best = jnp.maximum(best, part)

    @pl.when(place == 0)
    def _():
        best_ref[...] = best

    @pl.when(place > 0)
    def _():
        best_ref[...] = jnp.maximum(best_ref[...], best)

    @pl.when(place == PEAK_STEPS - 1)
    def _():
        peak_ref[...] = jnp.full(peak_ref.shape, jnp.max(best_ref[...]), jnp.float32)


def peak_call(view, devices):
    rows = view.shape[1]
    return pl.pallas_call(
        peak_kernel,
        grid=(PEAK_STEPS,),
        in_specs=[pl.BlockSpec((FIELDS, rows // PEAK_STEPS, 128, 128), lambda i: (0, i, 0, 0))],
        out_specs=pl.BlockSpec((devices, 128), lambda i: (0, 0)),
        out_shape=jax.ShapeDtypeStruct((devices, 128), jnp.float32),
        scratch_shapes=[pltpu.VMEM((8, 128), jnp.float32)],
        name="peak",
    )(view)


def border_kernel(high_ref, low_ref, peak_ref, up_ref, down_ref):
    up_ref[...] = high_ref[...]
    down_ref[...] = low_ref[...]


def border_call(view, peak):
    rows = view.shape[1]
    edge = jax.ShapeDtypeStruct((FIELDS, HALO, 128, 128), jnp.float32)
    block = (FIELDS, 1, 128, 128)
    return pl.pallas_call(
        border_kernel,
        grid=(HALO,),
        in_specs=[
            pl.BlockSpec(block, lambda i: (0, i + rows - HALO, 0, 0)),
            pl.BlockSpec(block, lambda i: (0, i, 0, 0)),
            pl.BlockSpec(memory_space=pl.ANY),
        ],
        out_specs=[pl.BlockSpec(block, lambda i: (0, i, 0, 0))] * 2,
        out_shape=[edge, edge],
        name="border",
    )(view, view, peak)


def turn(turned, slot, f, tile):
    flat = tile.T
    for v in range(128 // 8):
        place = (v % 2) * 64 + v // 2
        turned[slot, f, pl.ds(place, 8, stride=8), :] = flat[v * 8 : (v + 1) * 8]


def first_sweep(turned, slot, swept, row, scratch, half, beside):
    def cons(k):
        return [turned[slot, f, k * 8 : (k + 1) * 8, :] for f in range(FIELDS)]

    def put(k, new):
        for f in range(FIELDS):
            swept[f, row, k] = new[f]

    sweep_line(cons, put, scratch, SEGMENT, 1, half, True, beside)


def turn_back(final, row, back, slot, f):
    final[f, row] = back[slot, f].T


def last_sweep(done, row, back, slot, scratch, half, beside):
    def cons(k):
        return [done[f, row, k] for f in range(FIELDS)]

    def put(k, new):
        for f in range(FIELDS):
            back[slot, f, pl.ds(k, 8, stride=SEGMENT), :] = new[f]

    sweep_line(cons, put, scratch, SEGMENT, 1, half, True, beside)


def cross_sweep(swept, done, count, row, t, scratch, step):
    def cons(k):
        return [swept[f, k + HALO, t] for f in range(FIELDS)]

    def put(k, new):
        for f in range(FIELDS):
            done[f, k + row, t] = new[f]

    sweep_line(cons, put, scratch, count, 2, step, False)


def finish(done, final, back, scratch, half, count, row_out):
    def two_rows(i, carry):
        row = 2 * i
        earlier = jnp.maximum(row - 1, 0)
        last_sweep(
            done, row, back, 0, scratch, half, lambda f: turn_back(final, earlier, back, 1, f)
        )
        last_sweep(
            done, row + 1, back, 1, scratch, half, lambda f: turn_back(final, row, back, 0, f)
        )

        @pl.when(i > 0)
        def _():
            row_out(earlier).start()

        row_out(row).start()
        return carry

    lax.fori_loop(0, count // 2, two_rows, 0)
    for f in range(FIELDS):
        turn_back(final, count - 1, back, 1, f)
    row_out(count - 1).start()


def time_step(peaks_ref):
    peak = jnp.max(peaks_ref[...])
    step = courant_number / jnp.full((8, 128), peak, jnp.float32)
    return step, 0.5 * step


def inner_kernel(
    state_ref, peaks_ref, out_ref, rim_ref,
    raw, swept, done, final, turned, back, prim, face, courant, in_sems, out_sems, rim_sems,
):
    rows = state_ref.shape[1]
    inner = rows - 2 * HALO
    scratch = (prim, face, courant)

    def row_in(i):
        return pltpu.make_async_copy(state_ref.at[:, i], raw.at[:, i], in_sems.at[i])

    def row_out(i):
        return pltpu.make_async_copy(final.at[:, i], out_ref.at[:, i + HALO], out_sems.at[i])

    for i in range(rows):
        row_in(i).start()
    step, half = time_step(peaks_ref)
    row_in(0).wait()
    for f in range(FIELDS):
        turn(turned, 0, f, raw[f, 0])

    def two_rows(i, carry):
        row = 2 * i
        later = jnp.minimum(row + 2, rows - 1)
        row_in(row + 1).wait()

        @pl.when(row + 2 < rows)
        def _():
            row_in(later).wait()

        first_sweep(
            turned, 0, swept, row, scratch, half,
            lambda f: turn(turned, 1, f, raw[f, row + 1]),
        )
        first_sweep(
            turned, 1, swept, row + 1, scratch, half,
            lambda f: turn(turned, 0, f, raw[f, later]),
        )
        return carry

    lax.fori_loop(0, rows // 2, two_rows, 0)

    rims = (
        pltpu.make_async_copy(
            swept.at[:, pl.ds(0, 2 * HALO)], rim_ref.at[:, pl.ds(0, 2 * HALO)], rim_sems.at[0]
        ),
        pltpu.make_async_copy(
            swept.at[:, pl.ds(rows - 2 * HALO, 2 * HALO)],
            rim_ref.at[:, pl.ds(2 * HALO, 2 * HALO)],
            rim_sems.at[1],
        ),
    )
    for copy in rims:
        copy.start()

    def column(t, carry):
        cross_sweep(swept, done, inner, 0, t, scratch, step)
        return carry

    lax.fori_loop(0, SEGMENT, column, 0)
    finish(done, final, back, scratch, half, inner, row_out)
    for copy in rims:
        copy.wait()
    for i in range(inner):
        row_out(i).wait()


def outer_kernel(
    rim_ref, low_ref, high_ref, peaks_ref, half_done_ref, out_ref,
    raw, lower, upper, done, final, turned, back, prim, face, courant, in_sems, out_sems,
):
    rows = out_ref.shape[1]
    scratch = (prim, face, courant)
    copies = (
        pltpu.make_async_copy(low_ref, raw.at[:, pl.ds(0, HALO)], in_sems.at[0]),
        pltpu.make_async_copy(high_ref, raw.at[:, pl.ds(HALO, HALO)], in_sems.at[1]),
        pltpu.make_async_copy(
            rim_ref.at[:, pl.ds(0, 2 * HALO)], lower.at[:, pl.ds(HALO, 2 * HALO)], in_sems.at[2]
        ),
        pltpu.make_async_copy(
            rim_ref.at[:, pl.ds(2 * HALO, 2 * HALO)], upper.at[:, pl.ds(0, 2 * HALO)], in_sems.at[3]
        ),
    )

    def row_out(i):
        place = jnp.where(i < HALO, i, i + (rows - 2 * HALO))
        return pltpu.make_async_copy(final.at[:, i], out_ref.at[:, place], out_sems.at[i])

    for copy in copies:
        copy.start()
    step, half = time_step(peaks_ref)
    copies[0].wait()
    for f in range(FIELDS):
        turn(turned, 0, f, raw[f, 0])
    copies[1].wait()

    def two_rows(i, carry):
        later = jnp.minimum(i + 1, HALO - 1)
        first_sweep(
            turned, 0, lower, i, scratch, half,
            lambda f: turn(turned, 1, f, raw[f, i + HALO]),
        )
        first_sweep(
            turned, 1, upper, i + 2 * HALO, scratch, half,
            lambda f: turn(turned, 0, f, raw[f, later]),
        )
        return carry

    lax.fori_loop(0, HALO, two_rows, 0)
    copies[2].wait()
    copies[3].wait()

    def column(t, carry):
        cross_sweep(lower, done, HALO, 0, t, scratch, step)
        cross_sweep(upper, done, HALO, HALO, t, scratch, step)
        return carry

    lax.fori_loop(0, SEGMENT, column, 0)
    finish(done, final, back, scratch, half, 2 * HALO, row_out)
    for i in range(2 * HALO):
        row_out(i).wait()


def line_scratch(length):
    return [
        pltpu.VMEM((2, FIELDS, 128, 128), jnp.float32),
        pltpu.VMEM((2, FIELDS, 128, 128), jnp.float32),
        pltpu.VMEM((FIELDS, length + 2 * HALO, 8, 128), jnp.float32),
        pltpu.VMEM((2, FIELDS, length + 2 * HALO, 8, 128), jnp.float32),
        pltpu.VMEM((2, length + 2 * HALO, 8, 128), jnp.float32),
    ]


def inner_call(view, peaks):
    rows = view.shape[1]
    inner = rows - 2 * HALO
    anywhere = pl.BlockSpec(memory_space=pl.ANY)
    return pl.pallas_call(
        inner_kernel,
        in_specs=[anywhere, pl.BlockSpec(memory_space=pltpu.VMEM)],
        out_specs=[anywhere, anywhere],
        out_shape=[
            jax.ShapeDtypeStruct(view.shape, jnp.float32),
            jax.ShapeDtypeStruct((FIELDS, 4 * HALO, SEGMENT, 8, 128), jnp.float32),
        ],
        scratch_shapes=[
            pltpu.VMEM((FIELDS, rows, 128, 128), jnp.float32),
            pltpu.VMEM((FIELDS, rows, SEGMENT, 8, 128), jnp.float32),
            pltpu.VMEM((FIELDS, inner, SEGMENT, 8, 128), jnp.float32),
            pltpu.VMEM((FIELDS, inner, 128, 128), jnp.float32),
            *line_scratch(SEGMENT),
            pltpu.SemaphoreType.DMA((rows,)),
            pltpu.SemaphoreType.DMA((inner,)),
            pltpu.SemaphoreType.DMA((2,)),
        ],
        compiler_params=pltpu.CompilerParams(vmem_limit_bytes=48 * 1024 * 1024),
        name="inner",
    )(view, peaks)


def outer_call(rim, low, high, peaks, half_done):
    anywhere = pl.BlockSpec(memory_space=pl.ANY)
    return pl.pallas_call(
        outer_kernel,
        in_specs=[anywhere, anywhere, anywhere, pl.BlockSpec(memory_space=pltpu.VMEM), anywhere],
        out_specs=anywhere,
        out_shape=jax.ShapeDtypeStruct(half_done.shape, jnp.float32),
        input_output_aliases={4: 0},
        scratch_shapes=[
            pltpu.VMEM((FIELDS, 2 * HALO, 128, 128), jnp.float32),
            pltpu.VMEM((FIELDS, 3 * HALO, SEGMENT, 8, 128), jnp.float32),
            pltpu.VMEM((FIELDS, 3 * HALO, SEGMENT, 8, 128), jnp.float32),
            pltpu.VMEM((FIELDS, 2 * HALO, SEGMENT, 8, 128), jnp.float32),
            pltpu.VMEM((FIELDS, 2 * HALO, 128, 128), jnp.float32),
            *line_scratch(SEGMENT),
            pltpu.SemaphoreType.DMA((4,)),
            pltpu.SemaphoreType.DMA((2 * HALO,)),
        ],
        compiler_params=pltpu.CompilerParams(vmem_limit_bytes=48 * 1024 * 1024),
        name="outer",
    )(rim, low, high, peaks, half_done)


def local(state):
    fields, rows, planes, columns = state.shape
    tiles = columns // 128
    view = state.reshape(fields, rows, planes, tiles, 128).transpose(0, 1, 3, 2, 4)
    view = view.reshape(fields, rows, tiles * planes, 128)
    devices = 1
    for axis in WIDE_NARROW:
        devices *= lax.axis_size(axis)
    up = [(i, (i + 1) % devices) for i in range(devices)]
    peak = peak_call(view, devices)
    peaks = lax.all_to_all(peak, WIDE_NARROW, 0, 0, tiled=True)
    send_up, send_down = border_call(view, peaks)
    low = lax.ppermute(send_up, WIDE_NARROW, up)
    high = lax.ppermute(send_down, WIDE_NARROW, [(b, a) for a, b in up])
    out, rim = inner_call(view, peaks)
    out = outer_call(rim, low, high, peaks, out)
    out = out.reshape(fields, rows, tiles, planes, 128).transpose(0, 1, 3, 2, 4)
    return out.reshape(fields, rows, planes, columns)


def solution(mesh):
    split = Mesh(
        mesh.devices.reshape(4, 2, 2, 2, 4), ("wide_0", "wide_1", "wide_2", "narrow_0", "narrow_1")
    )
    placed = (P(None, WIDE_NARROW, None, None),)
    return jax.shard_map(
        local,
        mesh=split,
        in_specs=placed,
        out_specs=P(None, WIDE_NARROW, None, None),
        check_vma=False,
    )
```

```python
import jax
import jax.numpy as jnp
from jax import lax
from jax.experimental import pallas as pl
from jax.experimental.pallas import tpu as pltpu
from jax.sharding import Mesh
from jax.sharding import PartitionSpec as P

WIDE_NARROW = ("wide_0", "wide_1", "wide_2", "narrow_0", "narrow_1")

gamma_minus = 0.4
root_gamma = 1.4**0.5
courant_number = 0.6
smallest = 1e-30

FIELDS = 5
HALO = 3
SEGMENT = 16


def sound_speed(density, pressure, scale=1.0):
    return (root_gamma * scale) * (
        pressure * lax.rsqrt(jnp.maximum(pressure * density, smallest))
    )


def primitives(cons):
    density, mom_x, mom_y, mom_z, energy = cons
    inverse = 1.0 / density
    vel_x, vel_y, vel_z = mom_x * inverse, mom_y * inverse, mom_z * inverse
    kinetic = mom_x * vel_x + mom_y * vel_y + mom_z * vel_z
    pressure = gamma_minus * energy - (0.5 * gamma_minus) * kinetic
    return [density, vel_x, vel_y, vel_z, pressure]


def next_segment(value):
    moved = pltpu.roll(value, 7, 0)
    sub = lax.broadcasted_iota(jnp.int32, value.shape, 0)
    return jnp.where(sub == 7, pltpu.roll(moved, 124, 1), moved)


def last_segment(value):
    moved = pltpu.roll(value, 1, 0)
    sub = lax.broadcasted_iota(jnp.int32, value.shape, 0)
    return jnp.where(sub == 0, pltpu.roll(moved, 4, 1), moved)


class Lazy(dict):
    def __init__(self, make):
        super().__init__()
        self.make = make

    def __missing__(self, k):
        value = self[k] = self.make(k)
        return value


def make_reconstruct(cell, courant):
    def jump(k):
        step = cells[k + 1] - cells[k]
        return jnp.abs(step), step > 0

    def slope(k):
        (back, back_up), (fore, fore_up) = jumps[k - 1], jumps[k]
        turns = jnp.logical_xor(back_up, fore_up)
        size = jnp.minimum(back + fore, 4.0 * jnp.minimum(back, fore))
        return jnp.where(turns, 0.0, size), turns

    def edge(k):
        turn = slopes[k + 1][0] - slopes[k][0]
        base = 6.0 * jumps[k][0]
        return base - turn, base + turn

    def faces(k):
        right, left = edges[k][0], edges[k - 1][1]
        right, left = jnp.minimum(right, 2.0 * left), jnp.minimum(left, 2.0 * right)
        sigma, scale = courant(k)
        signed = jnp.where(slopes[k][1], 0.0, jnp.where(jumps[k][1], scale, -scale))
        right, left = signed * right, signed * left
        base = cells[k] - sigma * (right - left)
        return base + right, base - left

    cells, jumps, slopes, edges = Lazy(cell), Lazy(jump), Lazy(slope), Lazy(edge)
    return faces


def rusanov(before, behind, normal, step):
    half = 0.5 * step
    vn_l, vn_r = half * before[normal], half * behind[normal]
    speed = jnp.maximum(
        jnp.abs(vn_l) + sound_speed(before[0], before[4], half),
        jnp.abs(vn_r) + sound_speed(behind[0], behind[4], half),
    )
    rate_l, rate_r = vn_l + speed, vn_r - speed
    mass_l, mass_r = before[0] * rate_l, behind[0] * rate_r
    mom_l = [before[i] * mass_l for i in (1, 2, 3)]
    mom_r = [behind[i] * mass_r for i in (1, 2, 3)]
    kinetic = (
        (before[1] * mom_l[0] + before[2] * mom_l[1])
        + (before[3] * mom_l[2] + behind[1] * mom_r[0])
        + (behind[2] * mom_r[1] + behind[3] * mom_r[2])
    )
    flux = [mass_l + mass_r] + [mom_l[i] + mom_r[i] for i in range(3)]
    flux[normal] = flux[normal] + half * (before[4] + behind[4])
    flux.append(
        0.5 * kinetic
        + (before[4] * (2.5 * rate_l + vn_l) + behind[4] * (2.5 * rate_r + vn_r))
    )
    return flux


class Line:
    def __init__(self, cons, put, scratch, count, normal, step, wrap):
        self.cons, self.put, self.count, self.wrap = cons, put, count, wrap
        self.prim, self.face, self.courant = scratch
        self.normal, self.step = normal, step

    def ready(self):
        count = self.count

        def start(k):
            prim = primitives(self.cons(k))
            for f in range(FIELDS):
                self.prim[f, k + HALO] = prim[f]
            if self.wrap or -1 <= k <= count:
                sigma = self.step * jnp.abs(prim[self.normal]) + sound_speed(
                    prim[0], prim[4], self.step
                )
                self.courant[0, k + HALO] = sigma
                self.courant[1, k + HALO] = (1.0 / 12.0) - (1.0 / 12.0) * sigma
            return prim

        if not self.wrap:
            for k in range(-HALO, count + HALO):
                start(k)
            return
        for k in (0, 1):
            prim = start(k)
            for f in range(FIELDS):
                self.prim[f, count + k + HALO] = next_segment(prim[f])
        for k in (count - 2, count - 1):
            prim = start(k)
            for f in range(FIELDS):
                self.prim[f, k - count + HALO] = last_segment(prim[f])
        for k in range(2, count - 2):
            start(k)

    def rebuild(self, f):
        faces = make_reconstruct(
            lambda k: self.prim[f, k + HALO],
            lambda k: (self.courant[0, k + HALO], self.courant[1, k + HALO]),
        )
        order = [*range(2, self.count), 0, 1] if self.wrap else range(-1, self.count + 1)
        for k in order:
            self.face[0, f, k + HALO], self.face[1, f, k + HALO] = faces(k)

    def advance(self):
        count = self.count

        def flux(k, behind=None):
            before = [self.face[0, f, k + HALO] for f in range(FIELDS)]
            if behind is None:
                behind = [self.face[1, f, k + 1 + HALO] for f in range(FIELDS)]
            return rusanov(before, behind, self.normal, self.step)

        def update(k, low, high):
            old = self.cons(k)
            self.put(k, [old[f] + (low[f] - high[f]) for f in range(FIELDS)])

        if not self.wrap:
            low = flux(-1)
            for k in range(count):
                high = flux(k)
                update(k, low, high)
                low = high
            return
        behind = [next_segment(self.face[1, f, HALO]) for f in range(FIELDS)]
        front = low = flux(0)
        for k in range(1, count):
            if k == count // 2:
                end = flux(count - 1, behind)
                into = [last_segment(v) for v in end]
            high = flux(k) if k < count - 1 else end
            update(k, low, high)
            low = high
        update(0, into, front)


def in_turn(now, then, beside=None):
    for f in range(FIELDS):
        if beside is not None:
            beside(f)
        now.rebuild(f)
    then.ready()
    now.advance()


PEAK_STEPS = 4


def peak_kernel(state_ref, peak_ref, best_ref):
    rows = state_ref.shape[1]
    place = pl.program_id(0)

    def body(i, best):
        best = list(best)
        for row in range(rows):
            at = pl.ds(pl.multiple_of(i * 8, 8), 8)
            prim = primitives([state_ref[f, row, at, :] for f in range(FIELDS)])
            sound = sound_speed(prim[0], prim[4])
            new = jnp.maximum(jnp.abs(prim[1]), jnp.abs(prim[2])) + sound
            best[row] = jnp.maximum(best[row], new)
        return tuple(best)

    zero = jnp.zeros((8, 128), jnp.float32)
    parts = lax.fori_loop(0, 16, body, (zero,) * rows, unroll=4)
    best = parts[0]
    for part in parts[1:]:
        best = jnp.maximum(best, part)

    @pl.when(place == 0)
    def _():
        best_ref[...] = best

    @pl.when(place > 0)
    def _():
        best_ref[...] = jnp.maximum(best_ref[...], best)

    @pl.when(place == PEAK_STEPS - 1)
    def _():
        peak_ref[...] = jnp.full(peak_ref.shape, jnp.max(best_ref[...]), jnp.float32)


def peak_call(view, devices):
    rows = view.shape[1]
    return pl.pallas_call(
        peak_kernel,
        grid=(PEAK_STEPS,),
        in_specs=[pl.BlockSpec((FIELDS, rows // PEAK_STEPS, 128, 128), lambda i: (0, i, 0, 0))],
        out_specs=pl.BlockSpec((devices, 128), lambda i: (0, 0)),
        out_shape=jax.ShapeDtypeStruct((devices, 128), jnp.float32),
        scratch_shapes=[pltpu.VMEM((8, 128), jnp.float32)],
        name="peak",
    )(view)


def turn(place_ref, tile):
    flat = tile.T
    for v in range(128 // 8):
        place = (v % 2) * 64 + v // 2
        place_ref[pl.ds(place, 8, stride=8), :] = flat[v * 8 : (v + 1) * 8]


TURN_STEPS = 4


def turn_kernel(state_ref, turned_ref, up_ref, down_ref):
    rows = state_ref.shape[1]
    for row in range(rows):
        for f in range(FIELDS):
            turn(turned_ref.at[f, row], state_ref[f, row])

    @pl.when(pl.program_id(0) == 0)
    def _():
        for row in range(HALO):
            down_ref[:, row] = turned_ref[:, row]

    @pl.when(pl.program_id(0) == TURN_STEPS - 1)
    def _():
        for row in range(HALO):
            up_ref[:, row] = turned_ref[:, rows - HALO + row]


def turn_call(view):
    edge = (FIELDS, HALO, 128, 128)
    block = pl.BlockSpec(
        (FIELDS, view.shape[1] // TURN_STEPS, 128, 128), lambda i: (0, i, 0, 0)
    )
    return pl.pallas_call(
        turn_kernel,
        grid=(TURN_STEPS,),
        in_specs=[block],
        out_specs=[block] + [pl.BlockSpec(edge, lambda i: (0, 0, 0, 0))] * 2,
        out_shape=[
            jax.ShapeDtypeStruct(view.shape, jnp.float32),
            jax.ShapeDtypeStruct(edge, jnp.float32),
            jax.ShapeDtypeStruct(edge, jnp.float32),
        ],
        cost_estimate=pl.CostEstimate(flops=0, bytes_accessed=24 << 20, transcendentals=0),
        name="turn",
    )(view)


def first_line(turned, row, slot, swept, place, scratch, half):
    def cons(k):
        return [turned[f, row, k * 8 : (k + 1) * 8, :] for f in range(FIELDS)]

    def put(k, new):
        for f in range(FIELDS):
            swept[f, place, k] = new[f]

    return Line(cons, put, scratch[slot], SEGMENT, 1, half, True)


def last_line(done, row, back, slot, scratch, half):
    def cons(k):
        return [done[f, row, k] for f in range(FIELDS)]

    def put(k, new):
        for f in range(FIELDS):
            back[slot, f, pl.ds(k, 8, stride=SEGMENT), :] = new[f]

    return Line(cons, put, scratch[slot], SEGMENT, 1, half, True)


def cross_line(swept, done, count, row, t, slot, scratch, step):
    def cons(k):
        return [swept[f, k + HALO, t] for f in range(FIELDS)]

    def put(k, new):
        for f in range(FIELDS):
            done[f, k + row, t] = new[f]

    return Line(cons, put, scratch[slot], count, 2, step, False)


def finish(done, final, back, scratch, half, count, row_out):
    def line(row, slot):
        return last_line(done, row, back, slot, scratch, half)

    def turn_back(row, slot):
        def one(f):
            final[f, row] = back[slot, f].T

        return one

    line(0, 0).ready()

    def two_rows(i, carry):
        row = 2 * i
        earlier = jnp.maximum(row - 1, 0)
        later = jnp.minimum(row + 2, count - 1)
        in_turn(line(row, 0), line(row + 1, 1), turn_back(earlier, 1))
        in_turn(line(row + 1, 1), line(later, 0), turn_back(row, 0))

        @pl.when(i > 0)
        def _():
            row_out(earlier).start()

        row_out(row).start()
        return carry

    lax.fori_loop(0, count // 2, two_rows, 0)
    for f in range(FIELDS):
        turn_back(count - 1, 1)(f)
    row_out(count - 1).start()


def time_step(peaks_ref):
    peak = jnp.max(peaks_ref[...])
    step = courant_number / jnp.full((8, 128), peak, jnp.float32)
    return step, 0.5 * step


def inner_kernel(
    state_ref, peaks_ref, out_ref, rim_ref,
    raw, swept, done, final, back, prim, face, courant, in_sems, out_sems, rim_sems,
):
    rows = state_ref.shape[1]
    inner = rows - 2 * HALO
    scratch = [(prim.at[slot], face, courant.at[slot]) for slot in range(2)]

    def row_in(i):
        return pltpu.make_async_copy(state_ref.at[:, i], raw.at[:, i], in_sems.at[i])

    def row_out(i):
        return pltpu.make_async_copy(final.at[:, i], out_ref.at[:, i + HALO], out_sems.at[i])

    for i in range(rows):
        row_in(i).start()
    step, half = time_step(peaks_ref)

    def line(row, slot):
        return first_line(raw, row, slot, swept, row, scratch, half)

    row_in(0).wait()
    line(0, 0).ready()

    def two_rows(i, carry):
        row = 2 * i
        later = jnp.minimum(row + 2, rows - 1)
        row_in(row + 1).wait()

        @pl.when(row + 2 < rows)
        def _():
            row_in(later).wait()

        in_turn(line(row, 0), line(row + 1, 1))
        in_turn(line(row + 1, 1), line(later, 0))
        return carry

    lax.fori_loop(0, rows // 2, two_rows, 0)

    rims = (
        pltpu.make_async_copy(
            swept.at[:, pl.ds(0, 2 * HALO)], rim_ref.at[:, pl.ds(0, 2 * HALO)], rim_sems.at[0]
        ),
        pltpu.make_async_copy(
            swept.at[:, pl.ds(rows - 2 * HALO, 2 * HALO)],
            rim_ref.at[:, pl.ds(2 * HALO, 2 * HALO)],
            rim_sems.at[1],
        ),
    )
    for copy in rims:
        copy.start()

    def column(t, slot):
        return cross_line(swept, done, inner, 0, t, slot, scratch, step)

    column(0, 0).ready()

    def two_columns(i, carry):
        t = 2 * i
        in_turn(column(t, 0), column(t + 1, 1))
        in_turn(column(t + 1, 1), column(jnp.minimum(t + 2, SEGMENT - 1), 0))
        return carry

    lax.fori_loop(0, SEGMENT // 2, two_columns, 0)
    finish(done, final, back, scratch, half, inner, row_out)
    for copy in rims:
        copy.wait()
    for i in range(inner):
        row_out(i).wait()


def outer_kernel(
    rim_ref, low_ref, high_ref, peaks_ref, half_done_ref, out_ref,
    raw, lower, upper, done, final, back, prim, face, courant, in_sems, out_sems,
):
    rows = out_ref.shape[1]
    scratch = [(prim.at[slot], face, courant.at[slot]) for slot in range(2)]
    copies = (
        pltpu.make_async_copy(low_ref, raw.at[:, pl.ds(0, HALO)], in_sems.at[0]),
        pltpu.make_async_copy(high_ref, raw.at[:, pl.ds(HALO, HALO)], in_sems.at[1]),
        pltpu.make_async_copy(
            rim_ref.at[:, pl.ds(0, 2 * HALO)], lower.at[:, pl.ds(HALO, 2 * HALO)], in_sems.at[2]
        ),
        pltpu.make_async_copy(
            rim_ref.at[:, pl.ds(2 * HALO, 2 * HALO)], upper.at[:, pl.ds(0, 2 * HALO)], in_sems.at[3]
        ),
    )

    def row_out(i):
        place = jnp.where(i < HALO, i, i + (rows - 2 * HALO))
        return pltpu.make_async_copy(final.at[:, i], out_ref.at[:, place], out_sems.at[i])

    for copy in copies:
        copy.start()
    step, half = time_step(peaks_ref)
    copies[0].wait()
    copies[1].wait()

    def low_line(row):
        return first_line(raw, row, 0, lower, row, scratch, half)

    def high_line(row):
        return first_line(raw, row + HALO, 1, upper, row + 2 * HALO, scratch, half)

    low_line(0).ready()

    def two_rows(i, carry):
        in_turn(low_line(i), high_line(i))
        in_turn(high_line(i), low_line(jnp.minimum(i + 1, HALO - 1)))
        return carry

    lax.fori_loop(0, HALO, two_rows, 0)
    copies[2].wait()
    copies[3].wait()

    def low_column(t):
        return cross_line(lower, done, HALO, 0, t, 0, scratch, step)

    def high_column(t):
        return cross_line(upper, done, HALO, HALO, t, 1, scratch, step)

    low_column(0).ready()

    def column(t, carry):
        in_turn(low_column(t), high_column(t))
        in_turn(high_column(t), low_column(jnp.minimum(t + 1, SEGMENT - 1)))
        return carry

    lax.fori_loop(0, SEGMENT, column, 0)
    finish(done, final, back, scratch, half, 2 * HALO, row_out)
    for i in range(2 * HALO):
        row_out(i).wait()


def line_scratch(length):
    return [
        pltpu.VMEM((2, FIELDS, 128, 128), jnp.float32),
        pltpu.VMEM((2, FIELDS, length + 2 * HALO, 8, 128), jnp.float32),
        pltpu.VMEM((2, FIELDS, length + 2 * HALO, 8, 128), jnp.float32),
        pltpu.VMEM((2, 2, length + 2 * HALO, 8, 128), jnp.float32),
    ]


def inner_call(view, peaks):
    rows = view.shape[1]
    inner = rows - 2 * HALO
    anywhere = pl.BlockSpec(memory_space=pl.ANY)
    return pl.pallas_call(
        inner_kernel,
        in_specs=[anywhere, pl.BlockSpec(memory_space=pltpu.VMEM)],
        out_specs=[anywhere, anywhere],
        out_shape=[
            jax.ShapeDtypeStruct(view.shape, jnp.float32),
            jax.ShapeDtypeStruct((FIELDS, 4 * HALO, SEGMENT, 8, 128), jnp.float32),
        ],
        scratch_shapes=[
            pltpu.VMEM((FIELDS, rows, 128, 128), jnp.float32),
            pltpu.VMEM((FIELDS, rows, SEGMENT, 8, 128), jnp.float32),
            pltpu.VMEM((FIELDS, inner, SEGMENT, 8, 128), jnp.float32),
            pltpu.VMEM((FIELDS, inner, 128, 128), jnp.float32),
            *line_scratch(SEGMENT),
            pltpu.SemaphoreType.DMA((rows,)),
            pltpu.SemaphoreType.DMA((inner,)),
            pltpu.SemaphoreType.DMA((2,)),
        ],
        compiler_params=pltpu.CompilerParams(vmem_limit_bytes=48 * 1024 * 1024),
        name="inner",
    )(view, peaks)


def outer_call(rim, low, high, peaks, half_done):
    anywhere = pl.BlockSpec(memory_space=pl.ANY)
    return pl.pallas_call(
        outer_kernel,
        in_specs=[anywhere, anywhere, anywhere, pl.BlockSpec(memory_space=pltpu.VMEM), anywhere],
        out_specs=anywhere,
        out_shape=jax.ShapeDtypeStruct(half_done.shape, jnp.float32),
        input_output_aliases={4: 0},
        scratch_shapes=[
            pltpu.VMEM((FIELDS, 2 * HALO, 128, 128), jnp.float32),
            pltpu.VMEM((FIELDS, 3 * HALO, SEGMENT, 8, 128), jnp.float32),
            pltpu.VMEM((FIELDS, 3 * HALO, SEGMENT, 8, 128), jnp.float32),
            pltpu.VMEM((FIELDS, 2 * HALO, SEGMENT, 8, 128), jnp.float32),
            pltpu.VMEM((FIELDS, 2 * HALO, 128, 128), jnp.float32),
            *line_scratch(SEGMENT),
            pltpu.SemaphoreType.DMA((4,)),
            pltpu.SemaphoreType.DMA((2 * HALO,)),
        ],
        compiler_params=pltpu.CompilerParams(vmem_limit_bytes=48 * 1024 * 1024),
        name="outer",
    )(rim, low, high, peaks, half_done)


def local(state):
    fields, rows, planes, columns = state.shape
    tiles = columns // 128
    view = state.reshape(fields, rows, planes, tiles, 128).transpose(0, 1, 3, 2, 4)
    view = view.reshape(fields, rows, tiles * planes, 128)
    devices = 1
    for axis in WIDE_NARROW:
        devices *= lax.axis_size(axis)
    up = [(i, (i + 1) % devices) for i in range(devices)]
    peak = peak_call(view, devices)
    peaks = lax.all_to_all(peak, WIDE_NARROW, 0, 0, tiled=True)
    peaks, turned, send_up, send_down = lax.optimization_barrier((peaks, *turn_call(view)))
    low = lax.ppermute(send_up, WIDE_NARROW, up)
    high = lax.ppermute(send_down, WIDE_NARROW, [(b, a) for a, b in up])
    out, rim = inner_call(turned, peaks)
    out = outer_call(rim, low, high, peaks, out)
    out = out.reshape(fields, rows, tiles, planes, 128).transpose(0, 1, 3, 2, 4)
    return out.reshape(fields, rows, planes, columns)


def solution(mesh):
    split = Mesh(
        mesh.devices.reshape(4, 2, 2, 2, 4), ("wide_0", "wide_1", "wide_2", "narrow_0", "narrow_1")
    )
    placed = (P(None, WIDE_NARROW, None, None),)
    return jax.shard_map(
        local,
        mesh=split,
        in_specs=placed,
        out_specs=P(None, WIDE_NARROW, None, None),
        check_vma=False,
    )
```

```python
import jax
import jax.numpy as jnp
from jax import lax
from jax.experimental import pallas as pl
from jax.experimental.pallas import tpu as pltpu
from jax.sharding import Mesh
from jax.sharding import PartitionSpec as P

WIDE_NARROW = ("wide_0", "wide_1", "wide_2", "narrow_0", "narrow_1")

gamma_minus = 0.4
root_gamma = 1.4**0.5
courant_number = 0.6
smallest = 1e-30

FIELDS = 5
HALO = 3
SEGMENT = 16


def sound_speed(density, pressure, scale=1.0):
    return (root_gamma * scale) * (
        pressure * lax.rsqrt(jnp.maximum(pressure * density, smallest))
    )


def primitives(cons):
    density, mom_x, mom_y, mom_z, energy = cons
    inverse = 1.0 / density
    vel_x, vel_y, vel_z = mom_x * inverse, mom_y * inverse, mom_z * inverse
    kinetic = mom_x * vel_x + mom_y * vel_y + mom_z * vel_z
    pressure = gamma_minus * energy - (0.5 * gamma_minus) * kinetic
    return [density, vel_x, vel_y, vel_z, pressure]


def next_segment(value):
    moved = pltpu.roll(value, 7, 0)
    sub = lax.broadcasted_iota(jnp.int32, value.shape, 0)
    return jnp.where(sub == 7, pltpu.roll(moved, 124, 1), moved)


def last_segment(value):
    moved = pltpu.roll(value, 1, 0)
    sub = lax.broadcasted_iota(jnp.int32, value.shape, 0)
    return jnp.where(sub == 0, pltpu.roll(moved, 4, 1), moved)


class Lazy(dict):
    def __init__(self, make):
        super().__init__()
        self.make = make

    def __missing__(self, k):
        value = self[k] = self.make(k)
        return value


def make_reconstruct(cell, courant):
    def jump(k):
        step = cells[k + 1] - cells[k]
        return jnp.abs(step), step > 0

    def slope(k):
        (back, back_up), (fore, fore_up) = jumps[k - 1], jumps[k]
        turns = jnp.logical_xor(back_up, fore_up)
        size = jnp.minimum(back + fore, 4.0 * jnp.minimum(back, fore))
        return jnp.where(turns, 0.0, size), turns

    def edge(k):
        turn = slopes[k + 1][0] - slopes[k][0]
        base = 6.0 * jumps[k][0]
        return base - turn, base + turn

    def faces(k):
        right, left = edges[k][0], edges[k - 1][1]
        right, left = jnp.minimum(right, 2.0 * left), jnp.minimum(left, 2.0 * right)
        sigma, scale = courant(k)
        signed = jnp.where(slopes[k][1], 0.0, jnp.where(jumps[k][1], scale, -scale))
        right, left = signed * right, signed * left
        base = cells[k] - sigma * (right - left)
        return base + right, base - left

    cells, jumps, slopes, edges = Lazy(cell), Lazy(jump), Lazy(slope), Lazy(edge)
    return faces


def rusanov(before, behind, normal, step):
    half = 0.5 * step
    vn_l, vn_r = half * before[normal], half * behind[normal]
    speed = jnp.maximum(
        jnp.abs(vn_l) + sound_speed(before[0], before[4], half),
        jnp.abs(vn_r) + sound_speed(behind[0], behind[4], half),
    )
    rate_l, rate_r = vn_l + speed, vn_r - speed
    mass_l, mass_r = before[0] * rate_l, behind[0] * rate_r
    mom_l = [before[i] * mass_l for i in (1, 2, 3)]
    mom_r = [behind[i] * mass_r for i in (1, 2, 3)]
    kinetic = (
        (before[1] * mom_l[0] + before[2] * mom_l[1])
        + (before[3] * mom_l[2] + behind[1] * mom_r[0])
        + (behind[2] * mom_r[1] + behind[3] * mom_r[2])
    )
    flux = [mass_l + mass_r] + [mom_l[i] + mom_r[i] for i in range(3)]
    flux[normal] = flux[normal] + half * (before[4] + behind[4])
    flux.append(
        0.5 * kinetic
        + (before[4] * (2.5 * rate_l + vn_l) + behind[4] * (2.5 * rate_r + vn_r))
    )
    return flux


class Line:
    def __init__(self, cons, put, scratch, count, normal, step, wrap):
        self.cons, self.put, self.count, self.wrap = cons, put, count, wrap
        self.prim, self.face, self.courant = scratch
        self.normal, self.step = normal, step

    def ready(self):
        count = self.count

        def start(k):
            prim = primitives(self.cons(k))
            for f in range(FIELDS):
                self.prim[f, k + HALO] = prim[f]
            if self.wrap or -1 <= k <= count:
                sigma = self.step * jnp.abs(prim[self.normal]) + sound_speed(
                    prim[0], prim[4], self.step
                )
                self.courant[0, k + HALO] = sigma
                self.courant[1, k + HALO] = (1.0 / 12.0) - (1.0 / 12.0) * sigma
            return prim

        if not self.wrap:
            for k in range(-HALO, count + HALO):
                start(k)
            return
        for k in (0, 1):
            prim = start(k)
            for f in range(FIELDS):
                self.prim[f, count + k + HALO] = next_segment(prim[f])
        for k in (count - 2, count - 1):
            prim = start(k)
            for f in range(FIELDS):
                self.prim[f, k - count + HALO] = last_segment(prim[f])
        for k in range(2, count - 2):
            start(k)

    def rebuild(self, f):
        faces = make_reconstruct(
            lambda k: self.prim[f, k + HALO],
            lambda k: (self.courant[0, k + HALO], self.courant[1, k + HALO]),
        )
        order = [*range(2, self.count), 0, 1] if self.wrap else range(-1, self.count + 1)
        for k in order:
            self.face[0, f, k + HALO], self.face[1, f, k + HALO] = faces(k)

    def advance(self):
        count = self.count

        def flux(k, behind=None):
            before = [self.face[0, f, k + HALO] for f in range(FIELDS)]
            if behind is None:
                behind = [self.face[1, f, k + 1 + HALO] for f in range(FIELDS)]
            return rusanov(before, behind, self.normal, self.step)

        def update(k, low, high):
            old = self.cons(k)
            self.put(k, [old[f] + (low[f] - high[f]) for f in range(FIELDS)])

        if not self.wrap:
            low = flux(-1)
            for k in range(count):
                high = flux(k)
                update(k, low, high)
                low = high
            return
        behind = [next_segment(self.face[1, f, HALO]) for f in range(FIELDS)]
        front = low = flux(0)
        for k in range(1, count):
            if k == count // 2:
                end = flux(count - 1, behind)
                into = [last_segment(v) for v in end]
            high = flux(k) if k < count - 1 else end
            update(k, low, high)
            low = high
        update(0, into, front)


def in_turn(now, then, beside=None):
    for f in range(FIELDS):
        if beside is not None:
            beside(f)
        now.rebuild(f)
    then.ready()
    now.advance()


PEAK_ROWS = 2


def peak_kernel(state_ref, peak_ref, raw, sems):
    parts = state_ref.shape[1] // PEAK_ROWS

    def part_in(i):
        rows = pl.ds(i * PEAK_ROWS, PEAK_ROWS)
        return pltpu.make_async_copy(state_ref.at[:, rows], raw.at[:, rows], sems.at[i])

    for i in range(parts):
        part_in(i).start()

    def one_part(i, best):
        part_in(i).wait()
        best = list(best)
        for row in range(PEAK_ROWS):
            for k in range(16):
                at = slice(k * 8, (k + 1) * 8)
                prim = primitives([raw[f, i * PEAK_ROWS + row, at, :] for f in range(FIELDS)])
                sound = sound_speed(prim[0], prim[4])
                new = jnp.maximum(jnp.abs(prim[1]), jnp.abs(prim[2])) + sound
                best[k % 4] = jnp.maximum(best[k % 4], new)
        return tuple(best)

    zero = jnp.zeros((8, 128), jnp.float32)
    best = lax.fori_loop(0, parts, one_part, (zero,) * 4)
    best = jnp.maximum(jnp.maximum(best[0], best[1]), jnp.maximum(best[2], best[3]))
    peak_ref[...] = jnp.full(peak_ref.shape, jnp.max(best), jnp.float32)


def peak_call(view, devices):
    return pl.pallas_call(
        peak_kernel,
        in_specs=[pl.BlockSpec(memory_space=pl.ANY)],
        out_specs=pl.BlockSpec(memory_space=pltpu.VMEM),
        out_shape=jax.ShapeDtypeStruct((devices, 128), jnp.float32),
        scratch_shapes=[
            pltpu.VMEM(view.shape, jnp.float32),
            pltpu.SemaphoreType.DMA((view.shape[1] // PEAK_ROWS,)),
        ],
        name="peak",
    )(view)


def turn(place_ref, tile):
    flat = tile.T
    for v in range(128 // 8):
        place = (v % 2) * 64 + v // 2
        place_ref[pl.ds(place, 8, stride=8), :] = flat[v * 8 : (v + 1) * 8]


TURN_STEPS = 4


def turn_kernel(state_ref, turned_ref, up_ref, down_ref):
    rows = state_ref.shape[1]
    for row in range(rows):
        for f in range(FIELDS):
            turn(turned_ref.at[f, row], state_ref[f, row])

    @pl.when(pl.program_id(0) == 0)
    def _():
        for row in range(HALO):
            down_ref[:, row] = turned_ref[:, row]

    @pl.when(pl.program_id(0) == TURN_STEPS - 1)
    def _():
        for row in range(HALO):
            up_ref[:, row] = turned_ref[:, rows - HALO + row]


def turn_call(view):
    edge = (FIELDS, HALO, 128, 128)
    block = pl.BlockSpec(
        (FIELDS, view.shape[1] // TURN_STEPS, 128, 128), lambda i: (0, i, 0, 0)
    )
    return pl.pallas_call(
        turn_kernel,
        grid=(TURN_STEPS,),
        in_specs=[block],
        out_specs=[block] + [pl.BlockSpec(edge, lambda i: (0, 0, 0, 0))] * 2,
        out_shape=[
            jax.ShapeDtypeStruct(view.shape, jnp.float32),
            jax.ShapeDtypeStruct(edge, jnp.float32),
            jax.ShapeDtypeStruct(edge, jnp.float32),
        ],
        cost_estimate=pl.CostEstimate(flops=0, bytes_accessed=24 << 20, transcendentals=0),
        name="turn",
    )(view)


def first_line(turned, row, slot, swept, place, scratch, half):
    def cons(k):
        return [turned[f, row, k * 8 : (k + 1) * 8, :] for f in range(FIELDS)]

    def put(k, new):
        for f in range(FIELDS):
            swept[f, place, k] = new[f]

    return Line(cons, put, scratch[slot], SEGMENT, 1, half, True)


def last_line(done, row, back, slot, scratch, half):
    def cons(k):
        return [done[f, row, k] for f in range(FIELDS)]

    def put(k, new):
        for f in range(FIELDS):
            back[slot, f, pl.ds(k, 8, stride=SEGMENT), :] = new[f]

    return Line(cons, put, scratch[slot], SEGMENT, 1, half, True)


def cross_line(swept, done, count, row, t, slot, scratch, step):
    def cons(k):
        return [swept[f, k + HALO, t] for f in range(FIELDS)]

    def put(k, new):
        for f in range(FIELDS):
            done[f, k + row, t] = new[f]

    return Line(cons, put, scratch[slot], count, 2, step, False)


def finish(done, final, back, scratch, half, count, row_out):
    def line(row, slot):
        return last_line(done, row, back, slot, scratch, half)

    def turn_back(row, slot):
        def one(f):
            final[f, row] = back[slot, f].T

        return one

    line(0, 0).ready()

    def two_rows(i, carry):
        row = 2 * i
        earlier = jnp.maximum(row - 1, 0)
        later = jnp.minimum(row + 2, count - 1)
        in_turn(line(row, 0), line(row + 1, 1), turn_back(earlier, 1))
        in_turn(line(row + 1, 1), line(later, 0), turn_back(row, 0))

        @pl.when(i > 0)
        def _():
            row_out(earlier).start()

        row_out(row).start()
        return carry

    lax.fori_loop(0, count // 2, two_rows, 0)
    for f in range(FIELDS):
        turn_back(count - 1, 1)(f)
    row_out(count - 1).start()


def time_step(peaks_ref):
    peak = jnp.max(peaks_ref[...])
    step = courant_number / jnp.full((8, 128), peak, jnp.float32)
    return step, 0.5 * step


def inner_kernel(
    state_ref, peaks_ref, out_ref, rim_ref,
    raw, swept, done, final, back, prim, face, courant, in_sems, out_sems, rim_sems,
):
    rows = state_ref.shape[1]
    inner = rows - 2 * HALO
    scratch = [(prim.at[slot], face, courant.at[slot]) for slot in range(2)]

    def row_in(i):
        return pltpu.make_async_copy(state_ref.at[:, i], raw.at[:, i], in_sems.at[i])

    def row_out(i):
        return pltpu.make_async_copy(final.at[:, i], out_ref.at[:, i + HALO], out_sems.at[i])

    for i in range(rows):
        row_in(i).start()
    step, half = time_step(peaks_ref)

    def line(row, slot):
        return first_line(raw, row, slot, swept, row, scratch, half)

    row_in(0).wait()
    line(0, 0).ready()

    def two_rows(i, carry):
        row = 2 * i
        later = jnp.minimum(row + 2, rows - 1)
        row_in(row + 1).wait()

        @pl.when(row + 2 < rows)
        def _():
            row_in(later).wait()

        in_turn(line(row, 0), line(row + 1, 1))
        in_turn(line(row + 1, 1), line(later, 0))
        return carry

    lax.fori_loop(0, rows // 2, two_rows, 0)

    rims = (
        pltpu.make_async_copy(
            swept.at[:, pl.ds(0, 2 * HALO)], rim_ref.at[:, pl.ds(0, 2 * HALO)], rim_sems.at[0]
        ),
        pltpu.make_async_copy(
            swept.at[:, pl.ds(rows - 2 * HALO, 2 * HALO)],
            rim_ref.at[:, pl.ds(2 * HALO, 2 * HALO)],
            rim_sems.at[1],
        ),
    )
    for copy in rims:
        copy.start()

    def column(t, slot):
        return cross_line(swept, done, inner, 0, t, slot, scratch, step)

    column(0, 0).ready()

    def two_columns(i, carry):
        t = 2 * i
        in_turn(column(t, 0), column(t + 1, 1))
        in_turn(column(t + 1, 1), column(jnp.minimum(t + 2, SEGMENT - 1), 0))
        return carry

    lax.fori_loop(0, SEGMENT // 2, two_columns, 0)
    finish(done, final, back, scratch, half, inner, row_out)
    for copy in rims:
        copy.wait()
    for i in range(inner):
        row_out(i).wait()


def outer_kernel(
    rim_ref, low_ref, high_ref, peaks_ref, half_done_ref, out_ref,
    raw, lower, upper, done, final, back, prim, face, courant, in_sems, out_sems,
):
    rows = out_ref.shape[1]
    scratch = [(prim.at[slot], face, courant.at[slot]) for slot in range(2)]
    copies = (
        pltpu.make_async_copy(low_ref, raw.at[:, pl.ds(0, HALO)], in_sems.at[0]),
        pltpu.make_async_copy(high_ref, raw.at[:, pl.ds(HALO, HALO)], in_sems.at[1]),
        pltpu.make_async_copy(
            rim_ref.at[:, pl.ds(0, 2 * HALO)], lower.at[:, pl.ds(HALO, 2 * HALO)], in_sems.at[2]
        ),
        pltpu.make_async_copy(
            rim_ref.at[:, pl.ds(2 * HALO, 2 * HALO)], upper.at[:, pl.ds(0, 2 * HALO)], in_sems.at[3]
        ),
    )

    def row_out(i):
        place = jnp.where(i < HALO, i, i + (rows - 2 * HALO))
        return pltpu.make_async_copy(final.at[:, i], out_ref.at[:, place], out_sems.at[i])

    for copy in copies:
        copy.start()
    step, half = time_step(peaks_ref)
    copies[0].wait()
    copies[1].wait()

    def low_line(row):
        return first_line(raw, row, 0, lower, row, scratch, half)

    def high_line(row):
        return first_line(raw, row + HALO, 1, upper, row + 2 * HALO, scratch, half)

    low_line(0).ready()

    def two_rows(i, carry):
        in_turn(low_line(i), high_line(i))
        in_turn(high_line(i), low_line(jnp.minimum(i + 1, HALO - 1)))
        return carry

    lax.fori_loop(0, HALO, two_rows, 0)
    copies[2].wait()
    copies[3].wait()

    def low_column(t):
        return cross_line(lower, done, HALO, 0, t, 0, scratch, step)

    def high_column(t):
        return cross_line(upper, done, HALO, HALO, t, 1, scratch, step)

    low_column(0).ready()

    def two_columns(i, carry):
        t = 2 * i
        in_turn(low_column(t), high_column(t))
        in_turn(high_column(t), low_column(t + 1))
        in_turn(low_column(t + 1), high_column(t + 1))
        in_turn(high_column(t + 1), low_column(jnp.minimum(t + 2, SEGMENT - 1)))
        return carry

    lax.fori_loop(0, SEGMENT // 2, two_columns, 0)
    finish(done, final, back, scratch, half, 2 * HALO, row_out)
    for i in range(2 * HALO):
        row_out(i).wait()


def line_scratch(length):
    return [
        pltpu.VMEM((2, FIELDS, 128, 128), jnp.float32),
        pltpu.VMEM((2, FIELDS, length + 2 * HALO, 8, 128), jnp.float32),
        pltpu.VMEM((2, FIELDS, length + 2 * HALO, 8, 128), jnp.float32),
        pltpu.VMEM((2, 2, length + 2 * HALO, 8, 128), jnp.float32),
    ]


def inner_call(view, peaks):
    rows = view.shape[1]
    inner = rows - 2 * HALO
    anywhere = pl.BlockSpec(memory_space=pl.ANY)
    return pl.pallas_call(
        inner_kernel,
        in_specs=[anywhere, pl.BlockSpec(memory_space=pltpu.VMEM)],
        out_specs=[anywhere, anywhere],
        out_shape=[
            jax.ShapeDtypeStruct(view.shape, jnp.float32),
            jax.ShapeDtypeStruct((FIELDS, 4 * HALO, SEGMENT, 8, 128), jnp.float32),
        ],
        scratch_shapes=[
            pltpu.VMEM((FIELDS, rows, 128, 128), jnp.float32),
            pltpu.VMEM((FIELDS, rows, SEGMENT, 8, 128), jnp.float32),
            pltpu.VMEM((FIELDS, inner, SEGMENT, 8, 128), jnp.float32),
            pltpu.VMEM((FIELDS, inner, 128, 128), jnp.float32),
            *line_scratch(SEGMENT),
            pltpu.SemaphoreType.DMA((rows,)),
            pltpu.SemaphoreType.DMA((inner,)),
            pltpu.SemaphoreType.DMA((2,)),
        ],
        compiler_params=pltpu.CompilerParams(vmem_limit_bytes=48 * 1024 * 1024),
        name="inner",
    )(view, peaks)


def outer_call(rim, low, high, peaks, half_done):
    anywhere = pl.BlockSpec(memory_space=pl.ANY)
    return pl.pallas_call(
        outer_kernel,
        in_specs=[anywhere, anywhere, anywhere, pl.BlockSpec(memory_space=pltpu.VMEM), anywhere],
        out_specs=anywhere,
        out_shape=jax.ShapeDtypeStruct(half_done.shape, jnp.float32),
        input_output_aliases={4: 0},
        scratch_shapes=[
            pltpu.VMEM((FIELDS, 2 * HALO, 128, 128), jnp.float32),
            pltpu.VMEM((FIELDS, 3 * HALO, SEGMENT, 8, 128), jnp.float32),
            pltpu.VMEM((FIELDS, 3 * HALO, SEGMENT, 8, 128), jnp.float32),
            pltpu.VMEM((FIELDS, 2 * HALO, SEGMENT, 8, 128), jnp.float32),
            pltpu.VMEM((FIELDS, 2 * HALO, 128, 128), jnp.float32),
            *line_scratch(SEGMENT),
            pltpu.SemaphoreType.DMA((4,)),
            pltpu.SemaphoreType.DMA((2 * HALO,)),
        ],
        compiler_params=pltpu.CompilerParams(vmem_limit_bytes=48 * 1024 * 1024),
        name="outer",
    )(rim, low, high, peaks, half_done)


def local(state):
    fields, rows, planes, columns = state.shape
    tiles = columns // 128
    view = state.reshape(fields, rows, planes, tiles, 128).transpose(0, 1, 3, 2, 4)
    view = view.reshape(fields, rows, tiles * planes, 128)
    devices = 1
    for axis in WIDE_NARROW:
        devices *= lax.axis_size(axis)
    up = [(i, (i + 1) % devices) for i in range(devices)]
    peak = peak_call(view, devices)
    peaks = lax.all_to_all(peak, WIDE_NARROW, 0, 0, tiled=True)
    peaks, turned, send_up, send_down = lax.optimization_barrier((peaks, *turn_call(view)))
    low = lax.ppermute(send_up, WIDE_NARROW, up)
    high = lax.ppermute(send_down, WIDE_NARROW, [(b, a) for a, b in up])
    out, rim = inner_call(turned, peaks)
    out = outer_call(rim, low, high, peaks, out)
    out = out.reshape(fields, rows, tiles, planes, 128).transpose(0, 1, 3, 2, 4)
    return out.reshape(fields, rows, planes, columns)


def solution(mesh):
    split = Mesh(
        mesh.devices.reshape(4, 2, 2, 2, 4), ("wide_0", "wide_1", "wide_2", "narrow_0", "narrow_1")
    )
    placed = (P(None, WIDE_NARROW, None, None),)
    return jax.shard_map(
        local,
        mesh=split,
        in_specs=placed,
        out_specs=P(None, WIDE_NARROW, None, None),
        check_vma=False,
    )
```

```python
import jax
import jax.numpy as jnp
from jax import lax
from jax.experimental import pallas as pl
from jax.experimental.pallas import tpu as pltpu
from jax.sharding import Mesh
from jax.sharding import PartitionSpec as P

WIDE_NARROW = ("wide_0", "wide_1", "wide_2", "narrow_0", "narrow_1")

gamma_minus = 0.4
root_gamma = 1.4**0.5
courant_number = 0.6
smallest = 1e-30

FIELDS = 5
HALO = 3
SEGMENT = 16


def sound_speed(density, pressure, scale=1.0):
    return (root_gamma * scale) * (
        pressure * lax.rsqrt(jnp.maximum(pressure * density, smallest))
    )


def primitives(cons):
    density, mom_x, mom_y, mom_z, energy = cons
    inverse = 1.0 / density
    vel_x, vel_y, vel_z = mom_x * inverse, mom_y * inverse, mom_z * inverse
    kinetic = mom_x * vel_x + mom_y * vel_y + mom_z * vel_z
    pressure = gamma_minus * energy - (0.5 * gamma_minus) * kinetic
    return [density, vel_x, vel_y, vel_z, pressure]


def next_segment(value):
    moved = pltpu.roll(value, 7, 0)
    sub = lax.broadcasted_iota(jnp.int32, value.shape, 0)
    return jnp.where(sub == 7, pltpu.roll(moved, 124, 1), moved)


def last_segment(value):
    moved = pltpu.roll(value, 1, 0)
    sub = lax.broadcasted_iota(jnp.int32, value.shape, 0)
    return jnp.where(sub == 0, pltpu.roll(moved, 4, 1), moved)


class Lazy(dict):
    def __init__(self, make):
        super().__init__()
        self.make = make

    def __missing__(self, k):
        value = self[k] = self.make(k)
        return value


def make_reconstruct(cell, courant, closed=None):
    def jump(k):
        step = cells[k + 1] - cells[k]
        return jnp.abs(step), step > 0

    def slope(k):
        if closed is not None and k == -1:
            return last_segment(slopes[closed - 1][0]), None
        if closed is not None and k == closed:
            return next_segment(slopes[0][0]), None
        (back, back_up), (fore, fore_up) = jumps[k - 1], jumps[k]
        turns = jnp.logical_xor(back_up, fore_up)
        size = jnp.minimum(back + fore, 4.0 * jnp.minimum(back, fore))
        return jnp.where(turns, 0.0, size), turns

    def edge(k):
        turn = slopes[k + 1][0] - slopes[k][0]
        base = 6.0 * jumps[k][0]
        return base - turn, base + turn

    def faces(k):
        right, left = edges[k][0], edges[k - 1][1]
        right, left = jnp.minimum(right, 2.0 * left), jnp.minimum(left, 2.0 * right)
        sigma, scale = courant(k)
        signed = jnp.where(slopes[k][1], 0.0, jnp.where(jumps[k][1], scale, -scale))
        right, left = signed * right, signed * left
        base = cells[k] - sigma * (right - left)
        return base + right, base - left

    cells, jumps, slopes, edges = Lazy(cell), Lazy(jump), Lazy(slope), Lazy(edge)
    if closed is not None:
        slopes[closed], slopes[-1]
    return faces


def rusanov(before, behind, normal, step):
    half = 0.5 * step
    vn_l, vn_r = half * before[normal], half * behind[normal]
    speed = jnp.maximum(
        jnp.abs(vn_l) + sound_speed(before[0], before[4], half),
        jnp.abs(vn_r) + sound_speed(behind[0], behind[4], half),
    )
    rate_l, rate_r = vn_l + speed, vn_r - speed
    mass_l, mass_r = before[0] * rate_l, behind[0] * rate_r
    mom_l = [before[i] * mass_l for i in (1, 2, 3)]
    mom_r = [behind[i] * mass_r for i in (1, 2, 3)]
    kinetic = (
        (before[1] * mom_l[0] + before[2] * mom_l[1])
        + (before[3] * mom_l[2] + behind[1] * mom_r[0])
        + (behind[2] * mom_r[1] + behind[3] * mom_r[2])
    )
    flux = [mass_l + mass_r] + [mom_l[i] + mom_r[i] for i in range(3)]
    flux[normal] = flux[normal] + half * (before[4] + behind[4])
    flux.append(
        0.5 * kinetic
        + (before[4] * (2.5 * rate_l + vn_l) + behind[4] * (2.5 * rate_r + vn_r))
    )
    return flux


class Line:
    def __init__(self, cons, put, scratch, count, normal, step, wrap):
        self.cons, self.put, self.count, self.wrap = cons, put, count, wrap
        self.prim, self.face, self.courant = scratch
        self.normal, self.step = normal, step

    def ready(self):
        count = self.count

        def start(k):
            prim = primitives(self.cons(k))
            for f in range(FIELDS):
                self.prim[f, k + HALO] = prim[f]
            if self.wrap or -1 <= k <= count:
                sigma = self.step * jnp.abs(prim[self.normal]) + sound_speed(
                    prim[0], prim[4], self.step
                )
                self.courant[0, k + HALO] = sigma
                self.courant[1, k + HALO] = (1.0 / 12.0) - (1.0 / 12.0) * sigma
            return prim

        if not self.wrap:
            for k in range(-HALO, count + HALO):
                start(k)
            return
        prim = start(0)
        for f in range(FIELDS):
            self.prim[f, count + HALO] = next_segment(prim[f])
        prim = start(count - 1)
        for f in range(FIELDS):
            self.prim[f, HALO - 1] = last_segment(prim[f])
        for k in range(1, count - 1):
            start(k)

    def rebuild(self, f):
        faces = make_reconstruct(
            lambda k: self.prim[f, k + HALO],
            lambda k: (self.courant[0, k + HALO], self.courant[1, k + HALO]),
            self.count if self.wrap else None,
        )
        order = [*range(2, self.count), 0, 1] if self.wrap else range(-1, self.count + 1)
        for k in order:
            self.face[0, f, k + HALO], self.face[1, f, k + HALO] = faces(k)

    def advance(self):
        count = self.count

        def flux(k, behind=None):
            before = [self.face[0, f, k + HALO] for f in range(FIELDS)]
            if behind is None:
                behind = [self.face[1, f, k + 1 + HALO] for f in range(FIELDS)]
            return rusanov(before, behind, self.normal, self.step)

        def update(k, low, high):
            old = self.cons(k)
            self.put(k, [old[f] + (low[f] - high[f]) for f in range(FIELDS)])

        if not self.wrap:
            low = flux(-1)
            for k in range(count):
                high = flux(k)
                update(k, low, high)
                low = high
            return
        behind = [next_segment(self.face[1, f, HALO]) for f in range(FIELDS)]
        front = low = flux(0)
        for k in range(1, count):
            if k == count // 2:
                end = flux(count - 1, behind)
                into = [last_segment(v) for v in end]
            high = flux(k) if k < count - 1 else end
            update(k, low, high)
            low = high
        update(0, into, front)


def in_turn(now, then, beside=None):
    for f in range(FIELDS):
        if beside is not None:
            beside(f)
        now.rebuild(f)
    then.ready()
    now.advance()


PEAK_ROWS = 2


def peak_kernel(state_ref, peak_ref, raw, sems):
    parts = state_ref.shape[1] // PEAK_ROWS

    def part_in(i):
        rows = pl.ds(i * PEAK_ROWS, PEAK_ROWS)
        return pltpu.make_async_copy(state_ref.at[:, rows], raw.at[:, rows], sems.at[i])

    for i in range(parts):
        part_in(i).start()

    def one_part(i, best):
        part_in(i).wait()
        best = list(best)
        for row in range(PEAK_ROWS):
            for k in range(16):
                at = slice(k * 8, (k + 1) * 8)
                prim = primitives([raw[f, i * PEAK_ROWS + row, at, :] for f in range(FIELDS)])
                sound = sound_speed(prim[0], prim[4])
                new = jnp.maximum(jnp.abs(prim[1]), jnp.abs(prim[2])) + sound
                best[k % 4] = jnp.maximum(best[k % 4], new)
        return tuple(best)

    zero = jnp.zeros((8, 128), jnp.float32)
    best = lax.fori_loop(0, parts, one_part, (zero,) * 4)
    best = jnp.maximum(jnp.maximum(best[0], best[1]), jnp.maximum(best[2], best[3]))
    peak_ref[...] = jnp.full(peak_ref.shape, jnp.max(best), jnp.float32)


def peak_call(view, devices):
    return pl.pallas_call(
        peak_kernel,
        in_specs=[pl.BlockSpec(memory_space=pl.ANY)],
        out_specs=pl.BlockSpec(memory_space=pltpu.VMEM),
        out_shape=jax.ShapeDtypeStruct((devices, 128), jnp.float32),
        scratch_shapes=[
            pltpu.VMEM(view.shape, jnp.float32),
            pltpu.SemaphoreType.DMA((view.shape[1] // PEAK_ROWS,)),
        ],
        name="peak",
    )(view)


def turn(place_ref, tile):
    flat = tile.T
    for v in range(128 // 8):
        place = (v % 2) * 64 + v // 2
        place_ref[pl.ds(place, 8, stride=8), :] = flat[v * 8 : (v + 1) * 8]


TURN_STEPS = 4


def turn_kernel(state_ref, turned_ref, up_ref, down_ref):
    rows = state_ref.shape[1]
    for row in range(rows):
        for f in range(FIELDS):
            turn(turned_ref.at[f, row], state_ref[f, row])

    @pl.when(pl.program_id(0) == 0)
    def _():
        for row in range(HALO):
            down_ref[:, row] = turned_ref[:, row]

    @pl.when(pl.program_id(0) == TURN_STEPS - 1)
    def _():
        for row in range(HALO):
            up_ref[:, row] = turned_ref[:, rows - HALO + row]


def turn_call(view):
    edge = (FIELDS, HALO, 128, 128)
    block = pl.BlockSpec(
        (FIELDS, view.shape[1] // TURN_STEPS, 128, 128), lambda i: (0, i, 0, 0)
    )
    return pl.pallas_call(
        turn_kernel,
        grid=(TURN_STEPS,),
        in_specs=[block],
        out_specs=[block] + [pl.BlockSpec(edge, lambda i: (0, 0, 0, 0))] * 2,
        out_shape=[
            jax.ShapeDtypeStruct(view.shape, jnp.float32),
            jax.ShapeDtypeStruct(edge, jnp.float32),
            jax.ShapeDtypeStruct(edge, jnp.float32),
        ],
        cost_estimate=pl.CostEstimate(flops=0, bytes_accessed=24 << 20, transcendentals=0),
        name="turn",
    )(view)


def first_line(turned, row, slot, swept, place, scratch, half):
    def cons(k):
        return [turned[f, row, k * 8 : (k + 1) * 8, :] for f in range(FIELDS)]

    def put(k, new):
        for f in range(FIELDS):
            swept[f, place, k] = new[f]

    return Line(cons, put, scratch[slot], SEGMENT, 1, half, True)


def last_line(done, row, back, slot, scratch, half):
    def cons(k):
        return [done[f, row, k] for f in range(FIELDS)]

    def put(k, new):
        for f in range(FIELDS):
            back[slot, f, pl.ds(k, 8, stride=SEGMENT), :] = new[f]

    return Line(cons, put, scratch[slot], SEGMENT, 1, half, True)


def cross_line(swept, done, count, row, t, slot, scratch, step):
    def cons(k):
        return [swept[f, k + HALO, t] for f in range(FIELDS)]

    def put(k, new):
        for f in range(FIELDS):
            done[f, k + row, t] = new[f]

    return Line(cons, put, scratch[slot], count, 2, step, False)


def finish(done, final, back, scratch, half, count, row_out):
    def line(row, slot):
        return last_line(done, row, back, slot, scratch, half)

    def turn_back(row, slot):
        def one(f):
            final[f, row] = back[slot, f].T

        return one

    line(0, 0).ready()

    def two_rows(i, carry):
        row = 2 * i
        earlier = jnp.maximum(row - 1, 0)
        later = jnp.minimum(row + 2, count - 1)
        in_turn(line(row, 0), line(row + 1, 1), turn_back(earlier, 1))
        in_turn(line(row + 1, 1), line(later, 0), turn_back(row, 0))

        @pl.when(i > 0)
        def _():
            row_out(earlier).start()

        row_out(row).start()
        return carry

    lax.fori_loop(0, count // 2, two_rows, 0)
    for f in range(FIELDS):
        turn_back(count - 1, 1)(f)
    row_out(count - 1).start()


def time_step(peaks_ref):
    peak = jnp.max(peaks_ref[...])
    step = courant_number / jnp.full((8, 128), peak, jnp.float32)
    return step, 0.5 * step


def inner_kernel(
    state_ref, peaks_ref, out_ref, rim_ref,
    raw, swept, done, final, back, prim, face, courant, in_sems, out_sems, rim_sems,
):
    rows = state_ref.shape[1]
    inner = rows - 2 * HALO
    scratch = [(prim.at[slot], face, courant.at[slot]) for slot in range(2)]

    def row_in(i):
        return pltpu.make_async_copy(state_ref.at[:, i], raw.at[:, i], in_sems.at[i])

    def row_out(i):
        return pltpu.make_async_copy(final.at[:, i], out_ref.at[:, i + HALO], out_sems.at[i])

    for i in range(rows):
        row_in(i).start()
    step, half = time_step(peaks_ref)

    def line(row, slot):
        return first_line(raw, row, slot, swept, row, scratch, half)

    row_in(0).wait()
    line(0, 0).ready()

    def two_rows(i, carry):
        row = 2 * i
        later = jnp.minimum(row + 2, rows - 1)
        row_in(row + 1).wait()

        @pl.when(row + 2 < rows)
        def _():
            row_in(later).wait()

        in_turn(line(row, 0), line(row + 1, 1))
        in_turn(line(row + 1, 1), line(later, 0))
        return carry

    lax.fori_loop(0, rows // 2, two_rows, 0)

    rims = (
        pltpu.make_async_copy(
            swept.at[:, pl.ds(0, 2 * HALO)], rim_ref.at[:, pl.ds(0, 2 * HALO)], rim_sems.at[0]
        ),
        pltpu.make_async_copy(
            swept.at[:, pl.ds(rows - 2 * HALO, 2 * HALO)],
            rim_ref.at[:, pl.ds(2 * HALO, 2 * HALO)],
            rim_sems.at[1],
        ),
    )
    for copy in rims:
        copy.start()

    def column(t, slot):
        return cross_line(swept, done, inner, 0, t, slot, scratch, step)

    column(0, 0).ready()

    def two_columns(i, carry):
        t = 2 * i
        in_turn(column(t, 0), column(t + 1, 1))
        in_turn(column(t + 1, 1), column(jnp.minimum(t + 2, SEGMENT - 1), 0))
        return carry

    lax.fori_loop(0, SEGMENT // 2, two_columns, 0)
    finish(done, final, back, scratch, half, inner, row_out)
    for copy in rims:
        copy.wait()
    for i in range(inner):
        row_out(i).wait()


def outer_kernel(
    rim_ref, low_ref, high_ref, peaks_ref, half_done_ref, out_ref,
    raw, lower, upper, done, final, back, prim, face, courant, in_sems, out_sems,
):
    rows = out_ref.shape[1]
    scratch = [(prim.at[slot], face, courant.at[slot]) for slot in range(2)]
    copies = (
        pltpu.make_async_copy(low_ref, raw.at[:, pl.ds(0, HALO)], in_sems.at[0]),
        pltpu.make_async_copy(high_ref, raw.at[:, pl.ds(HALO, HALO)], in_sems.at[1]),
        pltpu.make_async_copy(
            rim_ref.at[:, pl.ds(0, 2 * HALO)], lower.at[:, pl.ds(HALO, 2 * HALO)], in_sems.at[2]
        ),
        pltpu.make_async_copy(
            rim_ref.at[:, pl.ds(2 * HALO, 2 * HALO)], upper.at[:, pl.ds(0, 2 * HALO)], in_sems.at[3]
        ),
    )

    def row_out(i):
        place = jnp.where(i < HALO, i, i + (rows - 2 * HALO))
        return pltpu.make_async_copy(final.at[:, i], out_ref.at[:, place], out_sems.at[i])

    for copy in copies:
        copy.start()
    step, half = time_step(peaks_ref)
    copies[0].wait()
    copies[1].wait()

    def low_line(row):
        return first_line(raw, row, 0, lower, row, scratch, half)

    def high_line(row):
        return first_line(raw, row + HALO, 1, upper, row + 2 * HALO, scratch, half)

    low_line(0).ready()

    def two_rows(i, carry):
        in_turn(low_line(i), high_line(i))
        in_turn(high_line(i), low_line(jnp.minimum(i + 1, HALO - 1)))
        return carry

    lax.fori_loop(0, HALO, two_rows, 0)
    copies[2].wait()
    copies[3].wait()

    def low_column(t):
        return cross_line(lower, done, HALO, 0, t, 0, scratch, step)

    def high_column(t):
        return cross_line(upper, done, HALO, HALO, t, 1, scratch, step)

    low_column(0).ready()

    def two_columns(i, carry):
        t = 2 * i
        in_turn(low_column(t), high_column(t))
        in_turn(high_column(t), low_column(t + 1))
        in_turn(low_column(t + 1), high_column(t + 1))
        in_turn(high_column(t + 1), low_column(jnp.minimum(t + 2, SEGMENT - 1)))
        return carry

    lax.fori_loop(0, SEGMENT // 2, two_columns, 0)
    finish(done, final, back, scratch, half, 2 * HALO, row_out)
    for i in range(2 * HALO):
        row_out(i).wait()


def line_scratch(length):
    return [
        pltpu.VMEM((2, FIELDS, 128, 128), jnp.float32),
        pltpu.VMEM((2, FIELDS, length + 2 * HALO, 8, 128), jnp.float32),
        pltpu.VMEM((2, FIELDS, length + 2 * HALO, 8, 128), jnp.float32),
        pltpu.VMEM((2, 2, length + 2 * HALO, 8, 128), jnp.float32),
    ]


def inner_call(view, peaks):
    rows = view.shape[1]
    inner = rows - 2 * HALO
    anywhere = pl.BlockSpec(memory_space=pl.ANY)
    return pl.pallas_call(
        inner_kernel,
        in_specs=[anywhere, pl.BlockSpec(memory_space=pltpu.VMEM)],
        out_specs=[anywhere, anywhere],
        out_shape=[
            jax.ShapeDtypeStruct(view.shape, jnp.float32),
            jax.ShapeDtypeStruct((FIELDS, 4 * HALO, SEGMENT, 8, 128), jnp.float32),
        ],
        scratch_shapes=[
            pltpu.VMEM((FIELDS, rows, 128, 128), jnp.float32),
            pltpu.VMEM((FIELDS, rows, SEGMENT, 8, 128), jnp.float32),
            pltpu.VMEM((FIELDS, inner, SEGMENT, 8, 128), jnp.float32),
            pltpu.VMEM((FIELDS, inner, 128, 128), jnp.float32),
            *line_scratch(SEGMENT),
            pltpu.SemaphoreType.DMA((rows,)),
            pltpu.SemaphoreType.DMA((inner,)),
            pltpu.SemaphoreType.DMA((2,)),
        ],
        compiler_params=pltpu.CompilerParams(vmem_limit_bytes=48 * 1024 * 1024),
        name="inner",
    )(view, peaks)


def outer_call(rim, low, high, peaks, half_done):
    anywhere = pl.BlockSpec(memory_space=pl.ANY)
    return pl.pallas_call(
        outer_kernel,
        in_specs=[anywhere, anywhere, anywhere, pl.BlockSpec(memory_space=pltpu.VMEM), anywhere],
        out_specs=anywhere,
        out_shape=jax.ShapeDtypeStruct(half_done.shape, jnp.float32),
        input_output_aliases={4: 0},
        scratch_shapes=[
            pltpu.VMEM((FIELDS, 2 * HALO, 128, 128), jnp.float32),
            pltpu.VMEM((FIELDS, 3 * HALO, SEGMENT, 8, 128), jnp.float32),
            pltpu.VMEM((FIELDS, 3 * HALO, SEGMENT, 8, 128), jnp.float32),
            pltpu.VMEM((FIELDS, 2 * HALO, SEGMENT, 8, 128), jnp.float32),
            pltpu.VMEM((FIELDS, 2 * HALO, 128, 128), jnp.float32),
            *line_scratch(SEGMENT),
            pltpu.SemaphoreType.DMA((4,)),
            pltpu.SemaphoreType.DMA((2 * HALO,)),
        ],
        compiler_params=pltpu.CompilerParams(vmem_limit_bytes=48 * 1024 * 1024),
        name="outer",
    )(rim, low, high, peaks, half_done)


def local(state):
    fields, rows, planes, columns = state.shape
    tiles = columns // 128
    view = state.reshape(fields, rows, planes, tiles, 128).transpose(0, 1, 3, 2, 4)
    view = view.reshape(fields, rows, tiles * planes, 128)
    devices = 1
    for axis in WIDE_NARROW:
        devices *= lax.axis_size(axis)
    up = [(i, (i + 1) % devices) for i in range(devices)]
    peak = peak_call(view, devices)
    peaks = lax.all_to_all(peak, WIDE_NARROW, 0, 0, tiled=True)
    peaks, turned, send_up, send_down = lax.optimization_barrier((peaks, *turn_call(view)))
    low = lax.ppermute(send_up, WIDE_NARROW, up)
    high = lax.ppermute(send_down, WIDE_NARROW, [(b, a) for a, b in up])
    out, rim = inner_call(turned, peaks)
    out = outer_call(rim, low, high, peaks, out)
    out = out.reshape(fields, rows, tiles, planes, 128).transpose(0, 1, 3, 2, 4)
    return out.reshape(fields, rows, planes, columns)


def solution(mesh):
    split = Mesh(
        mesh.devices.reshape(4, 2, 2, 2, 4), ("wide_0", "wide_1", "wide_2", "narrow_0", "narrow_1")
    )
    placed = (P(None, WIDE_NARROW, None, None),)
    return jax.shard_map(
        local,
        mesh=split,
        in_specs=placed,
        out_specs=P(None, WIDE_NARROW, None, None),
        check_vma=False,
    )
```
